256 devices in a mesh: dp: 128 (over x, z, y), mp: 2 (over core).
Axes of the slice: x: 4, y: 4, z: 8, core: 2. Of those that a mesh axis runs over, the one named last changes fastest.
Arguments:
- view_a: bfloat16 [16384, 4096], P(('dp', 'mp')), may hold values from -500 to 500
- view_b: bfloat16 [16384, 4096], P(('dp', 'mp')), may hold values from -500 to 500
Outputs:
- grad_a: bfloat16 [16384, 4096], P(('dp', 'mp'))
- grad_b: bfloat16 [16384, 4096], P(('dp', 'mp'))
The draws below stay inside these ranges and needn't reach their ends.
All inputs are finite; a program needn't handle non-finite values.
Results may differ from the reference program's by a relative error of at most 0.014.
Values may be sent and summed in bfloat16 or wider, within the bound.
A program may use at most 128 MiB of HBM per device.

```python
import jax
import jax.numpy as jnp
from jax import lax

D = 4096
PAIRS_DEV = 64
GROUPS_A = 8
GROUPS_B = 16
BATCH = 16384


def shared_signal(key):
    key_normal = jax.random.fold_in(key, 0)
    key_rows = jax.random.fold_in(key, 3)
    key_owner = jax.random.fold_in(key, 4)
    key_sign = jax.random.fold_in(key, 5)
    row_count = BATCH
    device_count = BATCH // PAIRS_DEV
    signal = jax.random.truncated_normal(key_normal, -4.0, 4.0, (row_count, D), jnp.float32)
    rising = 1.0 + 2.0 * jnp.arange(row_count, dtype=jnp.float32) / (row_count - 1)
    jitter = jax.random.uniform(key_rows, (row_count, 1), jnp.float32, 0.6, 1.6)
    owner = jax.random.randint(key_owner, (1, D), 0, device_count)
    sign_bits = jax.random.randint(key_sign, (1, D), 0, 2)
    signs = 2.0 * sign_bits.astype(jnp.float32) - 1.0
    row_owner = (jnp.arange(row_count, dtype=jnp.int32) // PAIRS_DEV)[:, None]
    height = 2.0 * jnp.sqrt(3.0 * device_count)
    block_offset = jnp.where(row_owner == owner, height * signs, 0.0)
    return (signal, rising[:, None] * jitter, block_offset)


def mixed_signal(key, signal, share_low, share_high):
    key_share, key_first, key_second, key_third = jax.random.split(key, 4)
    share = jnp.exp(jax.random.uniform(key_share, (1, D), jnp.float32, jnp.log(share_low), jnp.log(share_high)))
    total = signal[:, jax.random.permutation(key_first, D)]
    total = total + signal[:, jax.random.permutation(key_second, D)]
    total = total + signal[:, jax.random.permutation(key_third, D)]
    return jnp.sqrt(1.0 - share) * signal + jnp.sqrt(share / 3.0) * total


def make_view(key, signal, row_scales, block_offset):
    key_normal = jax.random.fold_in(key, 0)
    key_level = jax.random.fold_in(key, 2)
    key_scale = jax.random.fold_in(key, 3)
    key_center = jax.random.fold_in(key, 4)
    row_count = BATCH
    level = jnp.exp(jax.random.uniform(key_level, (1, D), jnp.float32, jnp.log(0.03), jnp.log(0.1)))
    noise = jax.random.truncated_normal(key_normal, -4.0, 4.0, (row_count, D), jnp.float32)
    feature_scale = jnp.exp(jax.random.uniform(key_scale, (1, D), jnp.float32, jnp.log(0.5), jnp.log(5.0)))
    feature_center = jax.random.uniform(key_center, (1, D), jnp.float32, -2.0, 2.0) * feature_scale
    return feature_center + feature_scale * (row_scales * (signal + level * noise) + block_offset)


def draw_view_a(key, part):
    signal, row_scales, block_offset = shared_signal(key)
    key = jax.random.fold_in(key, 11)
    return make_view(key, signal, row_scales, block_offset).astype(jnp.bfloat16)


def draw_view_b(key, part):
    signal, row_scales, block_offset = shared_signal(key)
    key = jax.random.fold_in(key, 23)
    coupled = mixed_signal(jax.random.fold_in(key, 5), signal, 0.1, 0.4)
    return make_view(key, coupled, row_scales, block_offset).astype(jnp.bfloat16)


def setup_inputs(seed: int = 0) -> dict:
    splits = jax.random.split(jax.random.key(seed), 3)
    view_a = draw_view_a(jax.random.fold_in(splits[2], 71), 0)
    view_b = draw_view_b(jax.random.fold_in(splits[2], 71), 0)
    return {"view_a": view_a, "view_b": view_b}


off_weight = 0.0051
epsilon = 1e-05
loss_scale = 16.0

def standardize(view):
    values = view.astype(jnp.float32)
    center = lax.optimization_barrier(jnp.mean(values, axis=0))
    shifted = values - center
    spread = lax.optimization_barrier(jnp.mean(shifted * shifted, axis=0))
    scaling = lax.rsqrt(spread + epsilon)
    return ((shifted * scaling).astype(jnp.bfloat16), scaling)

def reference(view_a, view_b):
    norm_a, rstd_a = standardize(view_a)
    norm_b, rstd_b = standardize(view_b)
    correlation = jnp.dot(norm_a.T, norm_b, preferred_element_type=jnp.float32) / BATCH
    row_ids = lax.broadcasted_iota(jnp.int32, (D, D), 0)
    col_ids = lax.broadcasted_iota(jnp.int32, (D, D), 1)
    grad_corr = jnp.where(row_ids == col_ids, -2.0 * (1.0 - correlation), 2.0 * off_weight * correlation).astype(jnp.bfloat16)
    width_a = D // GROUPS_A
    width_b = D // GROUPS_B
    back_a = jnp.zeros((BATCH, D), jnp.float32)
    for column_group in range(GROUPS_B):
        offset = column_group * width_b
        group_term = loss_scale * jnp.dot(norm_b[:, offset:offset + width_b], grad_corr[:, offset:offset + width_b].T, preferred_element_type=jnp.float32)
        back_a = back_a + lax.optimization_barrier(group_term.astype(jnp.bfloat16)).astype(jnp.float32)
    back_b = jnp.zeros((BATCH, D), jnp.float32)
    for row_group in range(GROUPS_A):
        offset = row_group * width_a
        group_term = loss_scale * jnp.dot(norm_a[:, offset:offset + width_a], grad_corr[offset:offset + width_a, :], preferred_element_type=jnp.float32)
        back_b = back_b + lax.optimization_barrier(group_term.astype(jnp.bfloat16)).astype(jnp.float32)
    float_a = norm_a.astype(jnp.float32)
    float_b = norm_b.astype(jnp.float32)
    moment_a = lax.optimization_barrier(jnp.mean(back_a * float_a, axis=0))
    moment_b = lax.optimization_barrier(jnp.mean(back_b * float_b, axis=0))
    grad_a = (rstd_a * (back_a - float_a * moment_a)).astype(jnp.bfloat16)
    grad_b = (rstd_b * (back_b - float_b * moment_b)).astype(jnp.bfloat16)
    return (grad_a, grad_b)
```

```python
import jax
import jax.numpy as jnp
from jax import lax
from jax.experimental import pallas as pl
from jax.experimental.pallas import tpu as pltpu
from jax.sharding import PartitionSpec as P

NX, NY, NZ, NC = 4, 4, 8, 2
R = 64
D = 4096
W = 1024
H = 512
Q = 128
N = 16384
OFF_WEIGHT = 0.0051
EPS = 1e-05
SCALE = 16.0
F32 = jnp.float32
BF16 = jnp.bfloat16
MESH = pl.DeviceIdType.MESH

_SIZES = dict(
    A=16, B=16, S1A=4, S1B=4, S2A=4, S2B=4, S3=16, CX=4,
    ZP=8, ZM=8, G=16, GX=16, MO=16, MA=4, MB=4,
    AP=6, AM=6, BP=6, BM=6, OA=4, OB=4, LOC=2,
)
SEM = {}
_n = 0
for _k, _v in _SIZES.items():
    SEM[_k] = _n
    _n += _v
N_RECV = _n
N_SEND = 260


def kernel(a_in, b_in, ga, gb, RA, RB, TA, TB, S0A, S0B, S1A, S1B, S2A, S2B, S3, FIN,
           CS, CO, CR, P0, P, M0, M, GT, MO, MA, MB, PA, PB, AP0, AP, AM0, AM, BP0, BP, BM0, BM,
           SA, SB, ssem, rsem):
    me = lax.axis_index("dp")
    c = lax.axis_index("mp")
    x = me // (NZ * NY)
    z = (me // NY) % NZ
    y = me % NY
    o = 1 - c

    def dev(xx, yy, zz, cc):
        return {"dp": xx * (NZ * NY) + zz * NY + yy, "mp": cc}

    def wrap(v, n):
        return (v + n) % n

    peers = [dev(wrap(x + k, NX), y, z, c) for k in range(1, NX)]
    peers += [dev(x, wrap(y + k, NY), z, c) for k in range(1, NY)]
    zc = [(k, s) for k in range(NZ) for s in range(NC) if (k, s) != (0, 0)]
    zc_peers = [dev(x, y, wrap(z + k, NZ), (c + s) % NC) for k, s in zc]
    peers += zc_peers
    barrier = pltpu.get_barrier_semaphore()
    for p in peers:
        pl.semaphore_signal(barrier, inc=1, device_id=p, device_id_type=MESH)
    pl.semaphore_wait(barrier, len(peers))

    xp, xm = dev(wrap(x + 1, NX), y, z, c), dev(wrap(x - 1, NX), y, z, c)
    yp, ym = dev(x, wrap(y + 1, NY), z, c), dev(x, wrap(y - 1, NY), z, c)
    zp, zm = dev(x, y, wrap(z + 1, NZ), c), dev(x, y, wrap(z - 1, NZ), c)
    sib = dev(x, y, z, o)

    sent = []

    def send(src, dst, fam, idx, to):
        cp = pltpu.make_async_remote_copy(
            src_ref=src, dst_ref=dst, send_sem=ssem.at[len(sent)], recv_sem=rsem.at[SEM[fam] + idx],
            device_id=to, device_id_type=MESH)
        cp.start()
        sent.append(cp)

    def recv(dst, fam, idx):
        pltpu.make_async_remote_copy(
            src_ref=dst, dst_ref=dst, send_sem=ssem.at[0], recv_sem=rsem.at[SEM[fam] + idx],
            device_id=sib, device_id_type=MESH).wait_recv()

    def cols(i, w=W):
        return pl.ds(pl.multiple_of(i * w, w), w)

    def slot(xx, yy):
        return xx * NY + yy

    def rows(s):
        return pl.ds(pl.multiple_of(s * R, R), R)

    own = slot(x, y)
    for k in (2, 1, 3):
        t = wrap(x + k, NX)
        send(a_in.at[:, cols(t)], RA.at[own], "A", own, dev(t, y, z, c))
        t = wrap(y + k, NY)
        send(b_in.at[:, cols(t)], RB.at[own], "B", own, dev(x, t, z, c))
    send(a_in.at[:, cols(x)], RA.at[own], "A", own, yp)
    send(a_in.at[:, cols(x)], RA.at[own], "A", own, ym)
    send(b_in.at[:, cols(y)], RB.at[own], "B", own, xp)
    send(b_in.at[:, cols(y)], RB.at[own], "B", own, xm)
    la = pltpu.make_async_copy(a_in.at[:, cols(x)], RA.at[own], rsem.at[SEM["LOC"]])
    lb = pltpu.make_async_copy(b_in.at[:, cols(y)], RB.at[own], rsem.at[SEM["LOC"] + 1])
    la.start()
    lb.start()

    def local_stats(v_ref, s_ref):
        for i in range(4):
            v = v_ref[:, i * W:(i + 1) * W].astype(F32)
            m = jnp.sum(v, axis=0, keepdims=True) * (1.0 / R)
            d = v - m
            s_ref[i, 0:1, :] = m
            s_ref[i, 1:2, :] = jnp.sum(d * d, axis=0, keepdims=True)

    local_stats(a_in, S0A)
    local_stats(b_in, S0B)
    for k in (2, 1, 3):
        t = wrap(x + k, NX)
        send(S0A.at[t], S1A.at[x], "S1A", x, dev(t, y, z, c))
        t = wrap(y + k, NY)
        send(S0B.at[t], S1B.at[y], "S1B", y, dev(x, t, z, c))
    S1A[x] = S0A[x]
    S1B[y] = S0B[y]

    def merge(parts, n):
        mean = parts[0][0]
        for m, _ in parts[1:]:
            mean = mean + m
        mean = mean * (1.0 / len(parts))
        total = None
        for m, q in parts:
            d = m - mean
            t = q + n * (d * d)
            total = t if total is None else total + t
        return mean, total

    la.wait()
    lb.wait()
    for k in (1, 3, 2):
        s = slot(wrap(x + k, NX), y)
        recv(RA.at[s], "A", s)
        send(RA.at[s], RA.at[s], "A", s, yp)
        send(RA.at[s], RA.at[s], "A", s, ym)
        s = slot(x, wrap(y + k, NY))
        recv(RB.at[s], "B", s)
        send(RB.at[s], RB.at[s], "B", s, xp)
        send(RB.at[s], RB.at[s], "B", s, xm)

    for k in (1, 3, 2):
        recv(S1A.at[wrap(x + k, NX)], "S1A", wrap(x + k, NX))
        recv(S1B.at[wrap(y + k, NY)], "S1B", wrap(y + k, NY))
    mean, m2 = merge([(S1A[k, 0:1, :], S1A[k, 1:2, :]) for k in range(4)], float(R))
    S2A[y, 0:1, :] = mean
    S2A[y, 1:2, :] = m2
    mean, m2 = merge([(S1B[k, 0:1, :], S1B[k, 1:2, :]) for k in range(4)], float(R))
    S2B[x, 0:1, :] = mean
    S2B[x, 1:2, :] = m2
    for k in (2, 1, 3):
        send(S2A.at[y], S2A.at[y], "S2A", y, dev(x, wrap(y + k, NY), z, c))
        send(S2B.at[x], S2B.at[x], "S2B", x, dev(wrap(x + k, NX), y, z, c))

    for k in (0, 1):
        s = slot(wrap(x + k, NX), wrap(y - 1, NY))
        recv(RA.at[s], "A", s)
        if k == 0:
            send(RA.at[s], RA.at[s], "A", s, yp)
        s = slot(wrap(x + k, NX), wrap(y + 1, NY))
        recv(RA.at[s], "A", s)
        if k == 1:
            send(RA.at[s], RA.at[s], "A", s, ym)
        s = slot(wrap(x - 1, NX), wrap(y + k, NY))
        recv(RB.at[s], "B", s)
        if k == 0:
            send(RB.at[s], RB.at[s], "B", s, xp)
        s = slot(wrap(x + 1, NX), wrap(y + k, NY))
        recv(RB.at[s], "B", s)
        if k == 1:
            send(RB.at[s], RB.at[s], "B", s, xm)

    for k in (1, 3, 2):
        recv(S2A.at[wrap(y + k, NY)], "S2A", wrap(y + k, NY))
        recv(S2B.at[wrap(x + k, NX)], "S2B", wrap(x + k, NX))
    mine = z * NC + c
    mean, m2 = merge([(S2A[k, 0:1, :], S2A[k, 1:2, :]) for k in range(4)], 4.0 * R)
    S3[mine, 0:1, :] = mean
    S3[mine, 1:2, :] = m2
    mean, m2 = merge([(S2B[k, 0:1, :], S2B[k, 1:2, :]) for k in range(4)], 4.0 * R)
    S3[mine, 2:3, :] = mean
    S3[mine, 3:4, :] = m2
    for p in zc_peers:
        send(S3.at[mine], S3.at[mine], "S3", mine, p)

    for k in (3, 2):
        s = slot(wrap(x + k, NX), wrap(y - 1, NY))
        recv(RA.at[s], "A", s)
        if k == 2:
            send(RA.at[s], RA.at[s], "A", s, yp)
        s = slot(wrap(x + k, NX), wrap(y + 1, NY))
        recv(RA.at[s], "A", s)
        if k == 3:
            send(RA.at[s], RA.at[s], "A", s, ym)
        s = slot(wrap(x - 1, NX), wrap(y + k, NY))
        recv(RB.at[s], "B", s)
        if k == 2:
            send(RB.at[s], RB.at[s], "B", s, xp)
        s = slot(wrap(x + 1, NX), wrap(y + k, NY))
        recv(RB.at[s], "B", s)
        if k == 3:
            send(RB.at[s], RB.at[s], "B", s, xm)

    for k, s in zc:
        i = wrap(z + k, NZ) * NC + (c + s) % NC
        recv(S3.at[i], "S3", i)
    for v in range(2):
        mean, m2 = merge([(S3[k, 2 * v:2 * v + 1, :], S3[k, 2 * v + 1:2 * v + 2, :]) for k in range(16)], 16.0 * R)
        FIN[2 * v:2 * v + 1, :] = mean
        FIN[2 * v + 1:2 * v + 2, :] = lax.rsqrt(m2 * (1.0 / N) + EPS)

    def norm_a(s):
        v = (RA[s].astype(F32) - FIN[0:1, :]) * FIN[1:2, :]
        TA[rows(s), :] = v.astype(BF16)

    def norm_b(s):
        v = (RB[s].astype(F32) - FIN[2:3, :]) * FIN[3:4, :]
        TB[rows(s), :] = v.astype(BF16)

    def early(i, _):
        k = i // 3
        h = (i % 3 + 3) % 4
        norm_a(slot(k, wrap(y + h, NY)))
        norm_b(slot(wrap(x + h, NX), k))
        return 0

    lax.fori_loop(0, 12, early, 0)
    for k in (0, 1, 3, 2):
        s = slot(wrap(x + k, NX), wrap(y + 2, NY))
        recv(RA.at[s], "A", s)
        norm_a(s)
        s = slot(wrap(x + 2, NX), wrap(y + k, NY))
        recv(RB.at[s], "B", s)
        norm_b(s)

    def corr(t, half):
        lhs = TA[:, cols(t, 2 * Q)]
        rhs = TB[:, cols(half, H)]
        return lax.dot_general(lhs, rhs, (((0,), (0,)), ((), ())), preferred_element_type=F32)

    def pair(t):
        return pl.ds(pl.multiple_of(t * 2, 2), 2)

    zt = z // 2
    for k in (2, 1, 3, 0):
        t = (zt + k) % 4
        CS[pair(t)] = corr(t, o).reshape(2, Q, H)
        send(CS.at[pair(t)], CR.at[pair(t)], "CX", t, sib)

    def own_half(k, _):
        t = (zt + k) % 4
        CO[pair(t)] = corr(t, c).reshape(2, Q, H)
        return 0

    lax.fori_loop(0, 4, own_half, 0)
    for k in (2, 1, 3, 0):
        t = (zt + k) % 4
        recv(CR.at[pair(t)], "CX", t)

    def add_other(k, _):
        CO[k] = CO[k] + CR[k]
        return 0

    lax.fori_loop(0, 8, add_other, 0)

    lo, hi = pl.ds(0, R), pl.ds(R, R)
    q4 = (z + 4) % NZ
    send(CO.at[q4, lo], P0, "ZP", 0, zp)
    send(CO.at[q4, hi], M0, "ZM", 0, zm)
    q3p, q3m = wrap(z + 3, NZ), wrap(z - 3, NZ)
    send(CO.at[q3p, hi], P.at[0, hi], "ZP", 1, zp)
    send(CO.at[q3m, lo], M.at[0, lo], "ZM", 1, zm)
    recv(P0, "ZP", 0)
    CO[q3p, lo] = CO[q3p, lo] + P0[...]
    send(CO.at[q3p, lo], P.at[0, lo], "ZP", 2, zp)
    recv(M0, "ZM", 0)
    CO[q3m, hi] = CO[q3m, hi] + M0[...]
    send(CO.at[q3m, hi], M.at[0, hi], "ZM", 2, zm)
    for j in (1, 2):
        qp, qm = wrap(z + 3 - j, NZ), wrap(z - 3 + j, NZ)
        for part, (sp, sm) in enumerate(((hi, lo), (lo, hi))):
            recv(P.at[j - 1, sp], "ZP", 2 * j - 1 + part)
            CO[qp, sp] = CO[qp, sp] + P[j - 1, sp]
            send(CO.at[qp, sp], P.at[j, sp], "ZP", 2 * j + 1 + part, zp)
            recv(M.at[j - 1, sm], "ZM", 2 * j - 1 + part)
            CO[qm, sm] = CO[qm, sm] + M[j - 1, sm]
            send(CO.at[qm, sm], M.at[j, sm], "ZM", 2 * j + 1 + part, zm)
    for part, (sp, sm) in enumerate(((hi, lo), (lo, hi))):
        recv(P.at[2, sp], "ZP", 5 + part)
        recv(M.at[2, sm], "ZM", 5 + part)
    cc = (CO[z] + (P[2] + M[2])) * (1.0 / N)

    ri = x * W + z * Q + lax.broadcasted_iota(jnp.int32, (Q, H), 0)
    ci = y * W + c * H + lax.broadcasted_iota(jnp.int32, (Q, H), 1)
    g = jnp.where(ri == ci, -2.0 * (1.0 - cc), (2.0 * OFF_WEIGHT) * cc).astype(BF16)
    GT[c, rowsq(z)] = g
    for part in (lo, hi):
        src = GT.at[c, pl.ds(pl.multiple_of(z * Q + part.start, R), R)]
        send(src, src, "G", 2 * z + part.start // R, zp)
        send(src, src, "G", 2 * z + part.start // R, zm)
    src = GT.at[c, rowsq(z)]
    send(src, src, "GX", c * NZ + z, sib)

    prod = g.astype(F32) * cc
    csum = jnp.sum(prod, axis=0, keepdims=True)
    for k in range(4):
        MO[mine, k:k + 1, :] = csum[:, k * 128:(k + 1) * 128]
    fold = prod[:, 0:128] + prod[:, 128:256] + prod[:, 256:384] + prod[:, 384:512]
    MO[mine, 4:5, :] = jnp.sum(fold.T, axis=0, keepdims=True)
    MO[mine, 5:8, :] = jnp.zeros((3, 128), F32)
    for p in zc_peers:
        send(MO.at[mine], MO.at[mine], "MO", mine, p)

    def gpart(q, h):
        return GT.at[c, pl.ds(pl.multiple_of(q * Q + h * R, R), R)]

    for j in (1, 2, 3):
        for sgn, to in ((-1, zp), (1, zm)):
            q = wrap(z + sgn * j, NZ)
            for h in (0, 1):
                recv(gpart(q, h), "G", 2 * q + h)
                if j < 3 or (h == 0 if sgn < 0 else h == 1):
                    send(gpart(q, h), gpart(q, h), "G", 2 * q + h, to)
            src = GT.at[c, rowsq(q)]
            send(src, src, "GX", c * NZ + q, sib)
    for h in (0, 1):
        recv(gpart(q4, h), "G", 2 * q4 + h)
    src = GT.at[c, rowsq(q4)]
    send(src, src, "GX", c * NZ + q4, sib)

    for k, s in zc:
        i = wrap(z + k, NZ) * NC + (c + s) % NC
        recv(MO.at[i], "MO", i)
    for q in range(NZ):
        MA[y, 0:1, q * Q:(q + 1) * Q] = MO[2 * q, 4:5, :] + MO[2 * q + 1, 4:5, :]
    for h in range(2):
        for k in range(4):
            t = MO[h, k:k + 1, :]
            for q in range(1, NZ):
                t = t + MO[2 * q + h, k:k + 1, :]
            MB[x, 0:1, h * H + k * 128:h * H + (k + 1) * 128] = t
    for k in (2, 1, 3):
        send(MA.at[y], MA.at[y], "MA", y, dev(x, wrap(y + k, NY), z, c))
        send(MB.at[x], MB.at[x], "MB", x, dev(wrap(x + k, NX), y, z, c))

    for q in range(NZ):
        qq = wrap(z - q, NZ)
        dst = GT.at[o, rowsq(qq)]
        recv(dst, "GX", o * NZ + qq)

    def term_a(yy):
        lhs = jnp.concatenate([TB[rows(slot(k, yy)), :] for k in range(4)], axis=0)
        t = lax.dot_general(lhs[:, :H], GT[0], (((1,), (1,)), ((), ())), preferred_element_type=F32)
        t = t + lax.dot_general(lhs[:, H:], GT[1], (((1,), (1,)), ((), ())), preferred_element_type=F32)
        return SCALE * t

    def term_b(xx):
        lhs = TA[pl.ds(pl.multiple_of(xx * 4 * R, 4 * R), 4 * R), :]
        return SCALE * jnp.concatenate(
            [jnp.dot(lhs, GT[h], preferred_element_type=F32) for h in range(2)], axis=1)

    sides = (
        (term_a, y, NY, PA, AP0, AP, AM0, AM, "AP", "AM", yp, ym),
        (term_b, x, NX, PB, BP0, BP, BM0, BM, "BP", "BM", xp, xm),
    )
    for term, pos, n, buf, p0, p1, m0, m1, fp, fm, to_p, to_m in sides:
        buf[2] = term(wrap(pos + 2, n)).astype(BF16).reshape(4, R, W)
        for k in range(2):
            send(buf.at[2, k], p0.at[k], fp, k, to_p)
            send(buf.at[2, 2 + k], m0.at[k], fm, k, to_m)
    for term, pos, n, buf, p0, p1, m0, m1, fp, fm, to_p, to_m in sides:
        buf[0] = term(wrap(pos + 1, n)).astype(BF16).reshape(4, R, W)
        for k in (2, 3):
            send(buf.at[0, k], p1.at[k], fp, 2 + k, to_p)
        for k in range(2):
            recv(p0.at[k], fp, k)
            buf[0, k] = (buf[0, k].astype(F32) + p0[k].astype(F32)).astype(BF16)
            send(buf.at[0, k], p1.at[k], fp, 2 + k, to_p)
        buf[1] = term(wrap(pos - 1, n)).astype(BF16).reshape(4, R, W)
        for k in range(2):
            send(buf.at[1, k], m1.at[k], fm, 2 + k, to_m)
        for k in range(2):
            recv(m0.at[k], fm, k)
            buf[1, 2 + k] = (buf[1, 2 + k].astype(F32) + m0[k].astype(F32)).astype(BF16)
            send(buf.at[1, 2 + k], m1.at[2 + k], fm, 4 + k, to_m)

    for k in (1, 3, 2):
        recv(MA.at[wrap(y + k, NY)], "MA", wrap(y + k, NY))
        recv(MB.at[wrap(x + k, NX)], "MB", wrap(x + k, NX))
    mom_a = ((MA[0] + MA[1]) + (MA[2] + MA[3])) * SCALE
    mom_b = ((MB[0] + MB[1]) + (MB[2] + MB[3])) * SCALE

    buf_a = term_a(y).astype(BF16)
    buf_b = term_b(x).astype(BF16)
    PA[3] = buf_a.reshape(4, R, W)
    PB[3] = buf_b.reshape(4, R, W)
    for k in range(4):
        recv(AP.at[k], "AP", 2 + k)
        recv(AM.at[k], "AM", 2 + k)
        back = PA[3, k].astype(F32) + (AP[k].astype(F32) + AM[k].astype(F32))
        SA[k] = (FIN[1:2, :] * (back - TA[rows(slot(k, y)), :].astype(F32) * mom_a)).astype(BF16)
        recv(BP.at[k], "BP", 2 + k)
        recv(BM.at[k], "BM", 2 + k)
        back = PB[3, k].astype(F32) + (BP[k].astype(F32) + BM[k].astype(F32))
        SB[k] = (FIN[3:4, :] * (back - TB[rows(slot(x, k)), :].astype(F32) * mom_b)).astype(BF16)
    for k in (2, 1, 3):
        t = wrap(x + k, NX)
        send(SA.at[t], ga.at[:, cols(x)], "OA", x, dev(t, y, z, c))
        t = wrap(y + k, NY)
        send(SB.at[t], gb.at[:, cols(y)], "OB", y, dev(x, t, z, c))
    ga[:, cols(x)] = SA[x]
    gb[:, cols(y)] = SB[y]
    for k in (1, 3, 2):
        t = wrap(x + k, NX)
        recv(ga.at[:, cols(t)], "OA", t)
        t = wrap(y + k, NY)
        recv(gb.at[:, cols(t)], "OB", t)
    for cp in sent:
        cp.wait_send()


def rowsq(q):
    return pl.ds(pl.multiple_of(q * Q, Q), Q)


def local(view_a, view_b):
    V = pltpu.VMEM
    scratch = [
        V((16, R, W), BF16), V((16, R, W), BF16),
        V((16 * R, W), BF16), V((16 * R, W), BF16),
        V((4, 2, W), F32), V((4, 2, W), F32),
        V((4, 2, W), F32), V((4, 2, W), F32),
        V((4, 2, W), F32), V((4, 2, W), F32),
        V((16, 4, W), F32), V((4, W), F32),
        V((NZ, Q, H), F32), V((NZ, Q, H), F32), V((NZ, Q, H), F32),
        V((R, H), F32), V((3, Q, H), F32), V((R, H), F32), V((3, Q, H), F32),
        V((2, W, H), BF16),
        V((16, 8, 128), F32), V((4, 1, W), F32), V((4, 1, W), F32),
        V((4, 4, R, W), BF16), V((4, 4, R, W), BF16),
        V((2, R, W), BF16), V((4, R, W), BF16), V((2, R, W), BF16), V((4, R, W), BF16),
        V((2, R, W), BF16), V((4, R, W), BF16), V((2, R, W), BF16), V((4, R, W), BF16),
        V((4, R, W), BF16), V((4, R, W), BF16),
        pltpu.SemaphoreType.DMA((N_SEND,)),
        pltpu.SemaphoreType.DMA((N_RECV,)),
    ]
    out = jax.ShapeDtypeStruct((R, D), BF16)
    return tuple(pl.pallas_call(
        kernel,
        out_shape=(out, out),
        in_specs=[pl.BlockSpec(memory_space=pltpu.VMEM)] * 2,
        out_specs=(pl.BlockSpec(memory_space=pltpu.VMEM),) * 2,
        scratch_shapes=scratch,
        compiler_params=pltpu.CompilerParams(
            collective_id=0, has_side_effects=True, vmem_limit_bytes=56 * 1024 * 1024),
    )(view_a, view_b))


def solution(mesh):
    spec = P(("dp", "mp"), None)
    return jax.shard_map(local, mesh=mesh, in_specs=(spec, spec), out_specs=(spec, spec), check_vma=False)
```

```python
import jax
import jax.numpy as jnp
from jax import lax
from jax.experimental import pallas as pl
from jax.experimental.pallas import tpu as pltpu
from jax.sharding import PartitionSpec as P

NX, NY, NZ, NC = 4, 4, 8, 2
R = 64
D = 4096
W = 1024
H = 512
Q = 128
N = 16384
OFF_WEIGHT = 0.0051
EPS = 1e-05
SCALE = 16.0
F32 = jnp.float32
BF16 = jnp.bfloat16
MESH = pl.DeviceIdType.MESH

_SIZES = dict(
    A=16, B=16, S1A=4, S1B=4, S2A=4, S2B=4, S3=16, CX=4,
    ZP=7, ZM=7, DV=8, G=16, GX=16, MO=16, MA=4, MB=4,
    AP=6, AM=6, BP=6, BM=6, OA=4, OB=4, LOC=2,
)
SEM = {}
_n = 0
for _k, _v in _SIZES.items():
    SEM[_k] = _n
    _n += _v
N_RECV = _n
N_SEND = 280


def kernel(a_hbm, b_hbm, ga, gb, a_in, b_in, RA, RB, TA, TB, S0A, S0B, S1A, S1B, S2A, S2B, S3, FIN,
           CS, CO, CR, P0, P, M0, M, ZP, ZM, DS, DV, GT, MO, MA, MB, PA, PB, AP0, AP, AM0, AM, BP0, BP, BM0, BM,
           SA, SB, ssem, rsem):
    me = lax.axis_index("dp")
    c = lax.axis_index("mp")
    x = me // (NZ * NY)
    z = (me // NY) % NZ
    y = me % NY
    o = 1 - c

    def dev(xx, yy, zz, cc):
        return {"dp": xx * (NZ * NY) + zz * NY + yy, "mp": cc}

    def wrap(v, n):
        return (v + n) % n

    peers = [dev(wrap(x + k, NX), y, z, c) for k in range(1, NX)]
    peers += [dev(x, wrap(y + k, NY), z, c) for k in range(1, NY)]
    zc = [(k, s) for k in range(NZ) for s in range(NC) if (k, s) != (0, 0)]
    zc_peers = [dev(x, y, wrap(z + k, NZ), (c + s) % NC) for k, s in zc]
    peers += zc_peers
    barrier = pltpu.get_barrier_semaphore()
    for p in peers:
        pl.semaphore_signal(barrier, inc=1, device_id=p, device_id_type=MESH)
    la = pltpu.make_async_copy(a_hbm, a_in, rsem.at[SEM["LOC"]])
    lb = pltpu.make_async_copy(b_hbm, b_in, rsem.at[SEM["LOC"] + 1])
    la.start()
    lb.start()

    xp, xm = dev(wrap(x + 1, NX), y, z, c), dev(wrap(x - 1, NX), y, z, c)
    yp, ym = dev(x, wrap(y + 1, NY), z, c), dev(x, wrap(y - 1, NY), z, c)
    zp, zm = dev(x, y, wrap(z + 1, NZ), c), dev(x, y, wrap(z - 1, NZ), c)
    sib = dev(x, y, z, o)

    sent = []

    def send(src, dst, fam, idx, to):
        cp = pltpu.make_async_remote_copy(
            src_ref=src, dst_ref=dst, send_sem=ssem.at[len(sent)], recv_sem=rsem.at[SEM[fam] + idx],
            device_id=to, device_id_type=MESH)
        cp.start()
        sent.append(cp)

    def recv(dst, fam, idx):
        pltpu.make_async_remote_copy(
            src_ref=dst, dst_ref=dst, send_sem=ssem.at[0], recv_sem=rsem.at[SEM[fam] + idx],
            device_id=sib, device_id_type=MESH).wait_recv()

    def cols(i, w=W):
        return pl.ds(pl.multiple_of(i * w, w), w)

    def slot(xx, yy):
        return xx * NY + yy

    def rows(s):
        return pl.ds(pl.multiple_of(s * R, R), R)

    def local_stats(v_ref, s_ref):
        for i in range(4):
            v = v_ref[:, i * W:(i + 1) * W].astype(F32)
            m = jnp.sum(v, axis=0, keepdims=True) * (1.0 / R)
            d = v - m
            s_ref[i, 0:1, :] = m
            s_ref[i, 1:2, :] = jnp.sum(d * d, axis=0, keepdims=True)

    own = slot(x, y)
    la.wait()
    local_stats(a_in, S0A)
    RA[own] = a_in[:, cols(x)]
    lb.wait()
    local_stats(b_in, S0B)
    RB[own] = b_in[:, cols(y)]
    pl.semaphore_wait(barrier, len(peers))

    for k in (2, 1, 3):
        t = wrap(x + k, NX)
        send(a_in.at[:, cols(t)], RA.at[own], "A", own, dev(t, y, z, c))
        t = wrap(y + k, NY)
        send(b_in.at[:, cols(t)], RB.at[own], "B", own, dev(x, t, z, c))
    send(a_in.at[:, cols(x)], RA.at[own], "A", own, yp)
    send(a_in.at[:, cols(x)], RA.at[own], "A", own, ym)
    send(b_in.at[:, cols(y)], RB.at[own], "B", own, xp)
    send(b_in.at[:, cols(y)], RB.at[own], "B", own, xm)
    for k in (2, 1, 3):
        t = wrap(x + k, NX)
        send(S0A.at[t], S1A.at[x], "S1A", x, dev(t, y, z, c))
        t = wrap(y + k, NY)
        send(S0B.at[t], S1B.at[y], "S1B", y, dev(x, t, z, c))
    S1A[x] = S0A[x]
    S1B[y] = S0B[y]

    def merge(parts, n):
        mean = parts[0][0]
        for m, _ in parts[1:]:
            mean = mean + m
        mean = mean * (1.0 / len(parts))
        total = None
        for m, q in parts:
            d = m - mean
            t = q + n * (d * d)
            total = t if total is None else total + t
        return mean, total

    for k in (1, 3, 2):
        s = slot(wrap(x + k, NX), y)
        recv(RA.at[s], "A", s)
        send(RA.at[s], RA.at[s], "A", s, yp)
        send(RA.at[s], RA.at[s], "A", s, ym)
        s = slot(x, wrap(y + k, NY))
        recv(RB.at[s], "B", s)
        send(RB.at[s], RB.at[s], "B", s, xp)
        send(RB.at[s], RB.at[s], "B", s, xm)

    for k in (1, 3, 2):
        recv(S1A.at[wrap(x + k, NX)], "S1A", wrap(x + k, NX))
        recv(S1B.at[wrap(y + k, NY)], "S1B", wrap(y + k, NY))
    mean, m2 = merge([(S1A[k, 0:1, :], S1A[k, 1:2, :]) for k in range(4)], float(R))
    S2A[y, 0:1, :] = mean
    S2A[y, 1:2, :] = m2
    mean, m2 = merge([(S1B[k, 0:1, :], S1B[k, 1:2, :]) for k in range(4)], float(R))
    S2B[x, 0:1, :] = mean
    S2B[x, 1:2, :] = m2
    for k in (2, 1, 3):
        send(S2A.at[y], S2A.at[y], "S2A", y, dev(x, wrap(y + k, NY), z, c))
        send(S2B.at[x], S2B.at[x], "S2B", x, dev(wrap(x + k, NX), y, z, c))

    for k in (0, 1):
        s = slot(wrap(x + k, NX), wrap(y - 1, NY))
        recv(RA.at[s], "A", s)
        if k == 0:
            send(RA.at[s], RA.at[s], "A", s, yp)
        s = slot(wrap(x + k, NX), wrap(y + 1, NY))
        recv(RA.at[s], "A", s)
        if k == 1:
            send(RA.at[s], RA.at[s], "A", s, ym)
        s = slot(wrap(x - 1, NX), wrap(y + k, NY))
        recv(RB.at[s], "B", s)
        if k == 0:
            send(RB.at[s], RB.at[s], "B", s, xp)
        s = slot(wrap(x + 1, NX), wrap(y + k, NY))
        recv(RB.at[s], "B", s)
        if k == 1:
            send(RB.at[s], RB.at[s], "B", s, xm)

    for k in (1, 3, 2):
        recv(S2A.at[wrap(y + k, NY)], "S2A", wrap(y + k, NY))
        recv(S2B.at[wrap(x + k, NX)], "S2B", wrap(x + k, NX))
    mine = z * NC + c
    mean, m2 = merge([(S2A[k, 0:1, :], S2A[k, 1:2, :]) for k in range(4)], 4.0 * R)
    S3[mine, 0:1, :] = mean
    S3[mine, 1:2, :] = m2
    mean, m2 = merge([(S2B[k, 0:1, :], S2B[k, 1:2, :]) for k in range(4)], 4.0 * R)
    S3[mine, 2:3, :] = mean
    S3[mine, 3:4, :] = m2
    for p in zc_peers:
        send(S3.at[mine], S3.at[mine], "S3", mine, p)

    for k in (3, 2):
        s = slot(wrap(x + k, NX), wrap(y - 1, NY))
        recv(RA.at[s], "A", s)
        if k == 2:
            send(RA.at[s], RA.at[s], "A", s, yp)
        s = slot(wrap(x + k, NX), wrap(y + 1, NY))
        recv(RA.at[s], "A", s)
        if k == 3:
            send(RA.at[s], RA.at[s], "A", s, ym)
        s = slot(wrap(x - 1, NX), wrap(y + k, NY))
        recv(RB.at[s], "B", s)
        if k == 2:
            send(RB.at[s], RB.at[s], "B", s, xp)
        s = slot(wrap(x + 1, NX), wrap(y + k, NY))
        recv(RB.at[s], "B", s)
        if k == 3:
            send(RB.at[s], RB.at[s], "B", s, xm)

    for k, s in zc:
        i = wrap(z + k, NZ) * NC + (c + s) % NC
        recv(S3.at[i], "S3", i)
    for v in range(2):
        mean, m2 = merge([(S3[k, 2 * v:2 * v + 1, :], S3[k, 2 * v + 1:2 * v + 2, :]) for k in range(16)], 16.0 * R)
        FIN[2 * v:2 * v + 1, :] = mean
        FIN[2 * v + 1:2 * v + 2, :] = lax.rsqrt(m2 * (1.0 / N) + EPS)

    def norm_a(s):
        v = (RA[s].astype(F32) - FIN[0:1, :]) * FIN[1:2, :]
        TA[rows(s), :] = v.astype(BF16)

    def norm_b(s):
        v = (RB[s].astype(F32) - FIN[2:3, :]) * FIN[3:4, :]
        TB[rows(s), :] = v.astype(BF16)

    def early(i, _):
        k = i // 3
        h = (i % 3 + 3) % 4
        norm_a(slot(k, wrap(y + h, NY)))
        norm_b(slot(wrap(x + h, NX), k))
        return 0

    lax.fori_loop(0, 12, early, 0)
    for k in (0, 1, 3, 2):
        s = slot(wrap(x + k, NX), wrap(y + 2, NY))
        recv(RA.at[s], "A", s)
        norm_a(s)
        s = slot(wrap(x + 2, NX), wrap(y + k, NY))
        recv(RB.at[s], "B", s)
        norm_b(s)

    def corr(t, half):
        lhs = TA[:, cols(t, 2 * Q)]
        rhs = TB[:, cols(half, H)]
        return lax.dot_general(lhs, rhs, (((0,), (0,)), ((), ())), preferred_element_type=F32)

    def pair(t):
        return pl.ds(pl.multiple_of(t * 2, 2), 2)

    zt = z // 2
    lo, hi = pl.ds(0, R), pl.ds(R, R)
    eye = (lax.broadcasted_iota(jnp.int32, (Q, Q), 0) == lax.broadcasted_iota(jnp.int32, (Q, Q), 1)).astype(F32)

    def give(k):
        t = (zt + k) % 4
        CS[pair(t)] = corr(t, o).reshape(2, Q, H)
        send(CS.at[pair(t)], CR.at[pair(t)], "CX", t, sib)

    def keep(k):
        t = (zt + k) % 4
        CO[pair(t)] = corr(t, c).reshape(2, Q, H)

    def add(k):
        t = (zt + k) % 4
        recv(CR.at[pair(t)], "CX", t)

        def body(i, _):
            q = 2 * t + i
            CO[q] = CO[q] + CR[q]
            block = CO[q, :, pl.ds(pl.multiple_of((q % 4) * Q, Q), Q)]
            DS[q] = jnp.sum(block * eye, axis=0, keepdims=True)
            return 0

        lax.fori_loop(0, 2, body, 0)

    q4 = (z + 4) % NZ
    zp2, zm2 = dev(x, y, wrap(z + 2, NZ), c), dev(x, y, wrap(z - 2, NZ), c)
    give(2)
    give(1)
    keep(2)
    give(3)
    add(2)
    ZP[3, lo] = CO[q4, lo].astype(BF16)
    send(ZP.at[3, lo], P0, "ZP", 0, zp2)
    ZM[3, hi] = CO[q4, hi].astype(BF16)
    send(ZM.at[3, hi], M0, "ZM", 0, zm2)
    keep(1)
    add(1)
    keep(3)
    add(3)
    for j in (0, 1, 2):
        qp, qm = wrap(z + 3 - j, NZ), wrap(z - 3 + j, NZ)
        for part, (sp, sm) in enumerate(((hi, lo), (lo, hi))):
            vp = CO[qp, sp]
            vm = CO[qm, sm]
            if j > 0:
                recv(P.at[j - 1, sp], "ZP", 2 * j - 1 + part)
                vp = vp + P[j - 1, sp].astype(F32)
            if j == 1 and part == 1:
                recv(P0, "ZP", 0)
                vp = vp + P0[...].astype(F32)
            ZP[j, sp] = vp.astype(BF16)
            send(ZP.at[j, sp], P.at[j, sp], "ZP", 2 * j + 1 + part, zp)
            if j > 0:
                recv(M.at[j - 1, sm], "ZM", 2 * j - 1 + part)
                vm = vm + M[j - 1, sm].astype(F32)
            if j == 1 and part == 1:
                recv(M0, "ZM", 0)
                vm = vm + M0[...].astype(F32)
            ZM[j, sm] = vm.astype(BF16)
            send(ZM.at[j, sm], M.at[j, sm], "ZM", 2 * j + 1 + part, zm)
        if j == 0:
            give(0)
            keep(0)
        if j == 1:
            add(0)
            for k in range(1, NZ):
                q = wrap(z + k, NZ)
                send(DS.at[q], DV.at[z], "DV", z, dev(x, y, q, c))
            DV[z] = DS[z]
    for k in range(1, NZ):
        q = wrap(z + k, NZ)
        recv(DV.at[q], "DV", q)
    dv = DV[0]
    for k in range(1, NZ):
        dv = dv + DV[k]
    diag = jnp.concatenate([dv] * 4, axis=1)
    for part, (sp, sm) in enumerate(((hi, lo), (lo, hi))):
        recv(P.at[2, sp], "ZP", 5 + part)
        recv(M.at[2, sm], "ZM", 5 + part)
    ri = x * W + z * Q + lax.broadcasted_iota(jnp.int32, (Q, H), 0)
    ci = y * W + c * H + lax.broadcasted_iota(jnp.int32, (Q, H), 1)
    cc = CO[z] + (P[2].astype(F32) + M[2].astype(F32))
    cc = jnp.where(ri == ci, diag, cc) * (1.0 / N)

    g = jnp.where(ri == ci, -2.0 * (1.0 - cc), (2.0 * OFF_WEIGHT) * cc).astype(BF16)
    GT[c, rowsq(z)] = g
    for first in (0, 1):
        for h, to in ((first, zp), (1 - first, zm)):
            src = GT.at[c, pl.ds(pl.multiple_of(z * Q + h * R, R), R)]
            send(src, src, "G", 2 * z + h, to)
    src = GT.at[c, rowsq(z)]
    send(src, src, "GX", c * NZ + z, sib)

    prod = g.astype(F32) * cc
    csum = jnp.sum(prod, axis=0, keepdims=True)
    for k in range(4):
        MO[mine, k:k + 1, :] = csum[:, k * 128:(k + 1) * 128]
    fold = prod[:, 0:128] + prod[:, 128:256] + prod[:, 256:384] + prod[:, 384:512]
    MO[mine, 4:5, :] = jnp.sum(fold.T, axis=0, keepdims=True)
    MO[mine, 5:8, :] = jnp.zeros((3, 128), F32)
    for p in zc_peers:
        send(MO.at[mine], MO.at[mine], "MO", mine, p)

    def gpart(q, h):
        return GT.at[c, pl.ds(pl.multiple_of(q * Q + h * R, R), R)]

    for j in (1, 2, 3):
        for sgn, to, to2, far in ((-1, zp, zp2, 0), (1, zm, zm2, 1)):
            q = wrap(z + sgn * j, NZ)
            for h in (far, 1 - far):
                recv(gpart(q, h), "G", 2 * q + h)
                if j < 3:
                    send(gpart(q, h), gpart(q, h), "G", 2 * q + h, to)
                if j == 2 and h == far:
                    send(gpart(q, h), gpart(q, h), "G", 2 * q + h, to2)
            src = GT.at[c, rowsq(q)]
            send(src, src, "GX", c * NZ + q, sib)
    for h in (0, 1):
        recv(gpart(q4, h), "G", 2 * q4 + h)
    src = GT.at[c, rowsq(q4)]
    send(src, src, "GX", c * NZ + q4, sib)

    for q in range(NZ):
        qq = wrap(z - q, NZ)
        dst = GT.at[o, rowsq(qq)]
        recv(dst, "GX", o * NZ + qq)

    order = (2, 1, 3, 0)

    def term_a(yy):
        lhs = jnp.concatenate([TB[rows(slot(wrap(x + r, NX), yy)), :] for r in order], axis=0)
        t = lax.dot_general(lhs[:, :H], GT[0], (((1,), (1,)), ((), ())), preferred_element_type=F32)
        t = t + lax.dot_general(lhs[:, H:], GT[1], (((1,), (1,)), ((), ())), preferred_element_type=F32)
        return SCALE * t

    def term_b(xx):
        lhs = jnp.concatenate([TA[rows(slot(xx, wrap(y + r, NY))), :] for r in order], axis=0)
        return SCALE * jnp.concatenate(
            [jnp.dot(lhs, GT[h], preferred_element_type=F32) for h in range(2)], axis=1)

    sides = (
        (term_a, y, NY, PA, AP0, AP, AM0, AM, "AP", "AM", yp, ym),
        (term_b, x, NX, PB, BP0, BP, BM0, BM, "BP", "BM", xp, xm),
    )
    for term, pos, n, buf, p0, p1, m0, m1, fp, fm, to_p, to_m in sides:
        buf[2] = term(wrap(pos + 2, n)).astype(BF16).reshape(4, R, W)
        for i, (kp, km) in enumerate(((0, 1), (3, 2))):
            send(buf.at[2, kp], p0.at[i], fp, i, to_p)
            send(buf.at[2, km], m0.at[i], fm, i, to_m)
    for k, s in zc:
        i = wrap(z + k, NZ) * NC + (c + s) % NC
        recv(MO.at[i], "MO", i)
    for q in range(NZ):
        MA[y, 0:1, q * Q:(q + 1) * Q] = MO[2 * q, 4:5, :] + MO[2 * q + 1, 4:5, :]
    for h in range(2):
        for k in range(4):
            t = MO[h, k:k + 1, :]
            for q in range(1, NZ):
                t = t + MO[2 * q + h, k:k + 1, :]
            MB[x, 0:1, h * H + k * 128:h * H + (k + 1) * 128] = t
    for k in (2, 1, 3):
        send(MA.at[y], MA.at[y], "MA", y, dev(x, wrap(y + k, NY), z, c))
        send(MB.at[x], MB.at[x], "MB", x, dev(wrap(x + k, NX), y, z, c))

    for term, pos, n, buf, p0, p1, m0, m1, fp, fm, to_p, to_m in sides:
        buf[0] = term(wrap(pos + 1, n)).astype(BF16).reshape(4, R, W)
        send(buf.at[0, 1], p1.at[1], fp, 3, to_p)
        buf[1] = term(wrap(pos - 1, n)).astype(BF16).reshape(4, R, W)
        send(buf.at[1, 0], m1.at[0], fm, 2, to_m)
    for i, (kp, km) in enumerate(((0, 1), (3, 2))):
        for term, pos, n, buf, p0, p1, m0, m1, fp, fm, to_p, to_m in sides:
            recv(p0.at[i], fp, i)
            buf[0, kp] = (buf[0, kp].astype(F32) + p0[i].astype(F32)).astype(BF16)
            send(buf.at[0, kp], p1.at[kp], fp, 2 + kp, to_p)
            recv(m0.at[i], fm, i)
            buf[1, km] = (buf[1, km].astype(F32) + m0[i].astype(F32)).astype(BF16)
            send(buf.at[1, km], m1.at[km], fm, 2 + km, to_m)
            if i == 0:
                send(buf.at[0, 2], p1.at[2], fp, 4, to_p)
                send(buf.at[1, 3], m1.at[3], fm, 5, to_m)

    for k in (1, 3, 2):
        recv(MA.at[wrap(y + k, NY)], "MA", wrap(y + k, NY))
        recv(MB.at[wrap(x + k, NX)], "MB", wrap(x + k, NX))
    mom_a = ((MA[0] + MA[1]) + (MA[2] + MA[3])) * SCALE
    mom_b = ((MB[0] + MB[1]) + (MB[2] + MB[3])) * SCALE

    buf_a = term_a(y).astype(BF16)
    buf_b = term_b(x).astype(BF16)
    PA[3] = buf_a.reshape(4, R, W)
    PB[3] = buf_b.reshape(4, R, W)
    for k, r in enumerate(order):
        recv(AP.at[k], "AP", 2 + k)
        recv(AM.at[k], "AM", 2 + k)
        t = wrap(x + r, NX)
        back = PA[3, k].astype(F32) + (AP[k].astype(F32) + AM[k].astype(F32))
        grad = (FIN[1:2, :] * (back - TA[rows(slot(t, y)), :].astype(F32) * mom_a)).astype(BF16)
        if r:
            SA[k] = grad
            send(SA.at[k], ga.at[:, cols(x)], "OA", x, dev(t, y, z, c))
        else:
            ga[:, cols(x)] = grad
        recv(BP.at[k], "BP", 2 + k)
        recv(BM.at[k], "BM", 2 + k)
        t = wrap(y + r, NY)
        back = PB[3, k].astype(F32) + (BP[k].astype(F32) + BM[k].astype(F32))
        grad = (FIN[3:4, :] * (back - TB[rows(slot(x, t)), :].astype(F32) * mom_b)).astype(BF16)
        if r:
            SB[k] = grad
            send(SB.at[k], gb.at[:, cols(y)], "OB", y, dev(x, t, z, c))
        else:
            gb[:, cols(y)] = grad
    for k in (1, 3, 2):
        t = wrap(x + k, NX)
        recv(ga.at[:, cols(t)], "OA", t)
        t = wrap(y + k, NY)
        recv(gb.at[:, cols(t)], "OB", t)
    for cp in sent:
        cp.wait_send()


def rowsq(q):
    return pl.ds(pl.multiple_of(q * Q, Q), Q)


def local(view_a, view_b):
    V = pltpu.VMEM
    scratch = [
        V((R, D), BF16), V((R, D), BF16),
        V((16, R, W), BF16), V((16, R, W), BF16),
        V((16 * R, W), BF16), V((16 * R, W), BF16),
        V((4, 2, W), F32), V((4, 2, W), F32),
        V((4, 2, W), F32), V((4, 2, W), F32),
        V((4, 2, W), F32), V((4, 2, W), F32),
        V((16, 4, W), F32), V((4, W), F32),
        V((NZ, Q, H), F32), V((NZ, Q, H), F32), V((NZ, Q, H), F32),
        V((R, H), BF16), V((3, Q, H), BF16), V((R, H), BF16), V((3, Q, H), BF16),
        V((4, Q, H), BF16), V((4, Q, H), BF16),
        V((NZ, 1, Q), F32), V((NZ, 1, Q), F32),
        V((2, W, H), BF16),
        V((16, 8, 128), F32), V((4, 1, W), F32), V((4, 1, W), F32),
        V((4, 4, R, W), BF16), V((4, 4, R, W), BF16),
        V((2, R, W), BF16), V((4, R, W), BF16), V((2, R, W), BF16), V((4, R, W), BF16),
        V((2, R, W), BF16), V((4, R, W), BF16), V((2, R, W), BF16), V((4, R, W), BF16),
        V((4, R, W), BF16), V((4, R, W), BF16),
        pltpu.SemaphoreType.DMA((N_SEND,)),
        pltpu.SemaphoreType.DMA((N_RECV,)),
    ]
    out = jax.ShapeDtypeStruct((R, D), BF16)
    return tuple(pl.pallas_call(
        kernel,
        out_shape=(out, out),
        in_specs=[pl.BlockSpec(memory_space=pl.ANY)] * 2,
        out_specs=(pl.BlockSpec(memory_space=pltpu.VMEM),) * 2,
        scratch_shapes=scratch,
        compiler_params=pltpu.CompilerParams(
            collective_id=0, has_side_effects=True, vmem_limit_bytes=56 * 1024 * 1024),
    )(view_a, view_b))


def solution(mesh):
    spec = P(("dp", "mp"), None)
    return jax.shard_map(local, mesh=mesh, in_specs=(spec, spec), out_specs=(spec, spec), check_vma=False)
```

```python
import jax
import jax.numpy as jnp
from jax import lax
from jax.experimental import pallas as pl
from jax.experimental.pallas import tpu as pltpu
from jax.sharding import PartitionSpec as P

NX, NY, NZ, NC = 4, 4, 8, 2
R = 64
D = 4096
W = 1024
E = 256
T = 16
BLOCKS = ((0, 0), (1, 0), (0, 1), (1, 1), (2, 0), (0, 2), (2, 1), (1, 2), (2, 2),
          (3, 0), (0, 3), (3, 1), (1, 3), (3, 2), (2, 3), (3, 3))
POS = {ij: p for p, ij in enumerate(BLOCKS)}
SETS = ((0, 4), (4, 6), (6, 9), (9, 11), (11, 13), (13, 16))
RECTS = (((0, 2, 0, 2),), ((2, 1, 0, 1), (0, 1, 2, 1)), ((2, 1, 1, 2), (1, 1, 2, 1)),
         ((3, 1, 0, 1), (0, 1, 3, 1)), ((3, 1, 1, 1), (1, 1, 3, 1)), ((3, 1, 2, 2), (2, 1, 3, 1)))
STEPS = ((0, 512), (512, 256), (768, 256))
N = 16384
OFF_WEIGHT = 0.0051
EPS = 1e-05
SCALE = 16.0
F32 = jnp.float32
BF16 = jnp.bfloat16
MESH = pl.DeviceIdType.MESH

_SIZES = dict(
    A1=12, B1=12, A2=24, B2=24, S1A=4, S1B=4, S2A=4, S2B=4, SC=1, S3=8, CX=6,
    Z1P=12, Z1M=12, ZHP=6, ZHM=6, Z2P=6, Z2M=6, DV=32, GF=48, GH=12, GX=6, MS=1, MO=8, MA=4, MB=4,
    BH=32, BF=32, OA=16, OB=16, LOC=2,
)
SEM = {}
_n = 0
for _k, _v in _SIZES.items():
    SEM[_k] = _n
    _n += _v
N_RECV = _n
N_SEND = 340


def kernel(a_hbm, b_hbm, ga, gb, a_in, b_in, RA0, RA1, RA2, RB0, RB1, RB2, TA, TB, S0A, S0B, S1A, S1B, S2A, S2B, SC, S3, FIN,
           TT, C2, CR, CO, Z1P, Z1M, ZHP, ZHM, Z2P, Z2M, Y1P, Y1M, YHP, YHM, Y2P, Y2M, DS, DV, GS, ACC, MS, MO, MA, MB,
           PB, BH, BF,
           SA, SB, ssem, rsem):
    me = lax.axis_index("dp")
    c = lax.axis_index("mp")
    x = me // (NZ * NY)
    z = (me // NY) % NZ
    y = me % NY
    o = 1 - c

    def dev(xx, yy, zz, cc):
        return {"dp": xx * (NZ * NY) + zz * NY + yy, "mp": cc}

    def wrap(v, n):
        return (v + n) % n

    peers = [dev(wrap(x + k, NX), y, z, c) for k in range(1, NX)]
    peers += [dev(x, wrap(y + k, NY), z, c) for k in range(1, NY)]
    peers += [dev(x, y, wrap(z + k, NZ), c) for k in range(1, NZ)]
    peers += [dev(x, y, z, 1 - c)]
    barrier = pltpu.get_barrier_semaphore()
    for p in peers:
        pl.semaphore_signal(barrier, inc=1, device_id=p, device_id_type=MESH)
    la = pltpu.make_async_copy(a_hbm, a_in, rsem.at[SEM["LOC"]])
    lb = pltpu.make_async_copy(b_hbm, b_in, rsem.at[SEM["LOC"] + 1])
    la.start()
    lb.start()

    xp, xm = dev(wrap(x + 1, NX), y, z, c), dev(wrap(x - 1, NX), y, z, c)
    yp, ym = dev(x, wrap(y + 1, NY), z, c), dev(x, wrap(y - 1, NY), z, c)
    zp, zm = dev(x, y, wrap(z + 1, NZ), c), dev(x, y, wrap(z - 1, NZ), c)
    sib = dev(x, y, z, o)

    RA, RB = (RA0, RA1, RA2), (RB0, RB1, RB2)
    sent = []

    def send(src, dst, fam, idx, to):
        cp = pltpu.make_async_remote_copy(
            src_ref=src, dst_ref=dst, send_sem=ssem.at[len(sent)], recv_sem=rsem.at[SEM[fam] + idx],
            device_id=to, device_id_type=MESH)
        cp.start()
        sent.append(cp)

    def recv(dst, fam, idx):
        pltpu.make_async_remote_copy(
            src_ref=dst, dst_ref=dst, send_sem=ssem.at[0], recv_sem=rsem.at[SEM[fam] + idx],
            device_id=sib, device_id_type=MESH).wait_recv()

    def cols(i, w=W):
        return pl.ds(pl.multiple_of(i * w, w), w)

    def part_of(i, off, w):
        return pl.ds(pl.multiple_of(i * W + off, w), w)

    def slot(xx, yy):
        return yy * NX + xx

    def rows(s):
        return pl.ds(pl.multiple_of(s * R, R), R)

    def local_stats(v_ref, s_ref):
        for i in range(4):
            v = v_ref[:, i * W:(i + 1) * W].astype(F32)
            m = jnp.sum(v, axis=0, keepdims=True) * (1.0 / R)
            d = v - m
            s_ref[i, 0:1, :] = m
            s_ref[i, 1:2, :] = jnp.sum(d * d, axis=0, keepdims=True)

    la.wait()
    local_stats(a_in, S0A)
    for (off, w), buf in zip(STEPS, RA):
        buf[y * 4 + x] = a_in[:, part_of(x, off, w)]
    lb.wait()
    local_stats(b_in, S0B)
    for (off, w), buf in zip(STEPS, RB):
        buf[x * 4 + y] = b_in[:, part_of(y, off, w)]
    pl.semaphore_wait(barrier, len(peers))

    def f1(n):
        off, w = STEPS[n]
        for k in (2, 1, 3):
            t = wrap(x + k, NX)
            send(a_in.at[:, part_of(t, off, w)], RA[n].at[y * 4 + x], "A1", 4 * n + x, dev(t, y, z, c))
            t = wrap(y + k, NY)
            send(b_in.at[:, part_of(t, off, w)], RB[n].at[x * 4 + y], "B1", 4 * n + y, dev(x, t, z, c))

    def two(buf, w, h):
        return buf.at[pl.ds(pl.multiple_of(w * 4 + 2 * h, 2), 2)]

    def f2(n):
        for k in (1, 3, 2):
            t = wrap(x + k, NX)
            recv(RA[n].at[y * 4 + t], "A1", 4 * n + t)
            t = wrap(y + k, NY)
            recv(RB[n].at[x * 4 + t], "B1", 4 * n + t)
        for h in (0, 1):
            for buf, fam, w, to_p, to_m in ((RA[n], "A2", y, yp, ym), (RB[n], "B2", x, xp, xm)):
                a, b = two(buf, w, h), two(buf, w, 1 - h)
                send(a, a, fam, 8 * n + 2 * w + h, to_p)
                send(b, b, fam, 8 * n + 2 * w + 1 - h, to_m)

    views = (("A2", y, NY, yp, ym), ("B2", x, NX, xp, xm))

    def fw(n):
        for (fam, w, size, to_p, to_m), buf in zip(views, (RA[n], RB[n])):
            for h, t, to in ((0, wrap(w - 1, size), to_p), (1, wrap(w + 1, size), to_m)):
                a = two(buf, t, h)
                recv(a, fam, 8 * n + 2 * t + h)
                send(a, a, fam, 8 * n + 2 * t + h, to)

    def norm(n, ta, tb):
        off, w = STEPS[n]
        cs = slice(off, off + w)

        def body(i, _):
            v = (RA[n][ta * 4 + i].astype(F32) - FIN[0:1, cs]) * FIN[1:2, cs]
            TA[rows(slot(i, ta)), cs] = v.astype(BF16)
            v = (RB[n][tb * 4 + i].astype(F32) - FIN[2:3, cs]) * FIN[3:4, cs]
            TB[rows(slot(tb, i)), cs] = v.astype(BF16)
            return 0

        lax.fori_loop(0, 4, body, 0)
        at = pl.ds(pl.multiple_of(ta * 4 * R, 4 * R), 4 * R)
        TT[cs, at] = TA[at, cs].T

    def rest(n):
        norm(n, y, x)
        for (fam, w, size, _, _), buf in zip(views, (RA[n], RB[n])):
            for h, t in ((1, wrap(w - 1, size)), (0, wrap(w + 1, size))):
                recv(two(buf, t, h), fam, 8 * n + 2 * t + h)
        norm(n, wrap(y - 1, NY), wrap(x - 1, NX))
        norm(n, wrap(y + 1, NY), wrap(x + 1, NX))
        for (fam, w, size, _, _), buf in zip(views, (RA[n], RB[n])):
            t = wrap(w + 2, size)
            for h in (0, 1):
                recv(two(buf, t, h), fam, 8 * n + 2 * t + h)
        norm(n, wrap(y + 2, NY), wrap(x + 2, NX))

    def merge(parts, n):
        mean = parts[0][0]
        for m, _ in parts[1:]:
            mean = mean + m
        mean = mean * (1.0 / len(parts))
        total = None
        for m, q in parts:
            d = m - mean
            t = q + n * (d * d)
            total = t if total is None else total + t
        return mean, total

    def st1():
        for k in (2, 1, 3):
            t = wrap(x + k, NX)
            send(S0A.at[t], S1A.at[x], "S1A", x, dev(t, y, z, c))
            t = wrap(y + k, NY)
            send(S0B.at[t], S1B.at[y], "S1B", y, dev(x, t, z, c))
        S1A[x] = S0A[x]
        S1B[y] = S0B[y]

    def st2():
        for k in (1, 3, 2):
            recv(S1A.at[wrap(x + k, NX)], "S1A", wrap(x + k, NX))
            recv(S1B.at[wrap(y + k, NY)], "S1B", wrap(y + k, NY))
        for src, dst, w in ((S1A, S2A, y), (S1B, S2B, x)):
            mean, m2 = merge([(src[k, 0:1, :], src[k, 1:2, :]) for k in range(4)], float(R))
            dst[w, 0:1, :] = mean
            dst[w, 1:2, :] = m2
        for k in (2, 1, 3):
            send(S2A.at[y], S2A.at[y], "S2A", y, dev(x, wrap(y + k, NY), z, c))
            send(S2B.at[x], S2B.at[x], "S2B", x, dev(wrap(x + k, NX), y, z, c))

    def st3():
        for k in (1, 3, 2):
            recv(S2A.at[wrap(y + k, NY)], "S2A", wrap(y + k, NY))
            recv(S2B.at[wrap(x + k, NX)], "S2B", wrap(x + k, NX))
        for v, src in ((0, S2A), (1, S2B)):
            mean, m2 = merge([(src[k, 0:1, :], src[k, 1:2, :]) for k in range(4)], 4.0 * R)
            SC[c, 2 * v:2 * v + 1, :] = mean
            SC[c, 2 * v + 1:2 * v + 2, :] = m2
        send(SC.at[c], SC.at[c], "SC", 0, sib)

    def st4():
        recv(SC.at[o], "SC", 0)
        for v in (0, 1):
            mean, m2 = merge([(SC[k, 2 * v:2 * v + 1, :], SC[k, 2 * v + 1:2 * v + 2, :]) for k in range(2)], 16.0 * R)
            S3[z, 2 * v:2 * v + 1, :] = mean
            S3[z, 2 * v + 1:2 * v + 2, :] = m2
        for k in (4, 3, 5, 2, 6, 1, 7):
            send(S3.at[z], S3.at[z], "S3", z, dev(x, y, wrap(z + k, NZ), c))

    def st5():
        for k in (1, 7, 2, 6, 3, 5, 4):
            recv(S3.at[wrap(z + k, NZ)], "S3", wrap(z + k, NZ))
        for v in (0, 1):
            mean, m2 = merge([(S3[k, 2 * v:2 * v + 1, :], S3[k, 2 * v + 1:2 * v + 2, :]) for k in range(8)], 32.0 * R)
            FIN[2 * v:2 * v + 1, :] = mean
            FIN[2 * v + 1:2 * v + 2, :] = lax.rsqrt(m2 * (1.0 / N) + EPS)

    def comp(n):
        p0, p1 = SETS[n]
        for i, ni, j, nj in RECTS[n]:
            t = jnp.dot(TT[i * E:(i + ni) * E, :], TB[:, j * E:(j + nj) * E], preferred_element_type=F32)
            for a in range(ni):
                for b in range(nj):
                    C2[POS[i + a, j + b]] = t[a * E:(a + 1) * E, b * E:(b + 1) * E].reshape(2, NZ, T, E)
        send(C2.at[p0:p1, o], CR.at[p0:p1], "CX", n, sib)

    zz = lax.broadcasted_iota(jnp.int32, (T, E), 1) - lax.broadcasted_iota(jnp.int32, (T, E), 0)

    def add(n):
        p0, p1 = SETS[n]
        recv(CR.at[p0:p1], "CX", n)

        def body(p, _):
            CO[p] = C2[p, c] + CR[p]
            return 0

        lax.fori_loop(p0, p1, body, 0)
        for p in range(p0, p1):
            i, j = BLOCKS[p]
            if i == j:
                for q in range(NZ):
                    DS[i, q] = jnp.sum(jnp.where(zz == c * 128 + q * T, CO[p, q], 0.0), axis=0, keepdims=True)

    zp2, zm2 = dev(x, y, wrap(z + 2, NZ), c), dev(x, y, wrap(z - 2, NZ), c)
    q4 = (z + 4) % NZ

    def rs1(n):
        p0, p1 = SETS[n]
        sl = slice(p0, p1)
        v = CO[sl, q4].astype(BF16)
        ZHP[sl] = v[:, :, :128]
        ZHM[sl] = v[:, :, 128:]
        send(ZHP.at[sl], YHP.at[sl], "ZHP", n, zp2)
        send(ZHM.at[sl], YHM.at[sl], "ZHM", n, zm2)
        for k in (1, 0):
            d = 1 + 2 * k
            Z1P[k, sl] = CO[sl, wrap(z + d, NZ)].astype(BF16)
            send(Z1P.at[k, sl], Y1P.at[k, sl], "Z1P", 2 * n + k, zp)
            Z1M[k, sl] = CO[sl, wrap(z - d, NZ)].astype(BF16)
            send(Z1M.at[k, sl], Y1M.at[k, sl], "Z1M", 2 * n + k, zm)
        for p in range(p0, p1):
            i, j = BLOCKS[p]
            if i == j:
                for k in range(1, NZ):
                    q = wrap(z + k, NZ)
                    send(DS.at[i, q], DV.at[i, z], "DV", i * NZ + z, dev(x, y, q, c))
                DV[i, z] = DS[i, z]

    def rs2(n):
        sl = slice(*SETS[n])
        recv(YHP.at[sl], "ZHP", n)
        recv(Y1P.at[1, sl], "Z1P", 2 * n + 1)
        v = CO[sl, wrap(z + 2, NZ)] + Y1P[1, sl].astype(F32)
        h = YHP[sl].astype(F32)
        Z2P[sl] = jnp.concatenate([v[:, :, :128] + h, v[:, :, 128:]], axis=2).astype(BF16)
        send(Z2P.at[sl], Y2P.at[sl], "Z2P", n, zp2)
        recv(YHM.at[sl], "ZHM", n)
        recv(Y1M.at[1, sl], "Z1M", 2 * n + 1)
        v = CO[sl, wrap(z - 2, NZ)] + Y1M[1, sl].astype(F32)
        h = YHM[sl].astype(F32)
        Z2M[sl] = jnp.concatenate([v[:, :, :128], v[:, :, 128:] + h], axis=2).astype(BF16)
        send(Z2M.at[sl], Y2M.at[sl], "Z2M", n, zm2)

    def fin(n):
        p0, p1 = SETS[n]
        sl = slice(p0, p1)
        recv(Y1P.at[0, sl], "Z1P", 2 * n)
        recv(Y1M.at[0, sl], "Z1M", 2 * n)
        recv(Y2P.at[sl], "Z2P", n)
        recv(Y2M.at[sl], "Z2M", n)
        for p in range(p0, p1):
            i, j = BLOCKS[p]
            cc = CO[p, z] + ((Y1P[0, p].astype(F32) + Y1M[0, p].astype(F32)) + (Y2P[p].astype(F32) + Y2M[p].astype(F32)))
            if i == j:
                dv = DV[i, z]
                for k in range(1, NZ):
                    q = wrap(z + k, NZ)
                    recv(DV.at[i, q], "DV", i * NZ + q)
                    dv = dv + DV[i, q]
                on = jnp.logical_and(zz == c * 128 + z * T, x == y)
                cc = jnp.where(on, dv, cc) * (1.0 / N)
                g = jnp.where(on, -2.0 * (1.0 - cc), (2.0 * OFF_WEIGHT) * cc).astype(BF16)
            else:
                cc = cc * (1.0 / N)
                g = ((2.0 * OFF_WEIGHT) * cc).astype(BF16)
            GS[p, c, z] = g
            prod = g.astype(F32) * cc
            ACC[0, i] = ACC[0, i] + prod
            ACC[1, j] = ACC[1, j] + prod
        src = GS.at[sl, c, z]
        for k, to in ((0, zp), (2, zm)):
            send(src, src, "GF", 8 * n + k, to)

    def ag1(n):
        sl = slice(*SETS[n])
        for k, q, to in ((0, wrap(z - 1, NZ), zp), (2, wrap(z + 1, NZ), zm)):
            src = GS.at[sl, c, q]
            recv(src, "GF", 8 * n + k)
            send(src, src, "GF", 8 * n + k + 1, to)

    lanes_p, lanes_m = slice(0, 128), slice(128, 256)

    def ag2(n):
        sl = slice(*SETS[n])
        for k, q, to, to2, lanes in ((1, wrap(z - 2, NZ), zp, zp2, lanes_p), (3, wrap(z + 2, NZ), zm, zm2, lanes_m)):
            src = GS.at[sl, c, q]
            recv(src, "GF", 8 * n + k)
            half = GS.at[sl, c, q, :, lanes]
            send(half, half, "GH", 2 * n + k // 2, to2)
            send(src, src, "GF", 8 * n + 4 + k, to)

    def gx(n):
        sl = slice(*SETS[n])
        for k, q in ((5, wrap(z - 3, NZ)), (7, wrap(z + 3, NZ))):
            recv(GS.at[sl, c, q], "GF", 8 * n + k)
        recv(GS.at[sl, c, q4, :, lanes_p], "GH", 2 * n)
        recv(GS.at[sl, c, q4, :, lanes_m], "GH", 2 * n + 1)
        send(GS.at[sl, c], GS.at[sl, c], "GX", n, sib)

    def gx_wait(n):
        sl = slice(*SETS[n])
        recv(GS.at[sl, o], "GX", n)

    def mom1():
        for i in range(4):
            r = jnp.sum(ACC[0, i], axis=1, keepdims=True)
            MS[c, 0:1, i * E:(i + 1) * E] = jnp.sum(jnp.where(zz == c * 128 + z * T, r, 0.0), axis=0, keepdims=True)
            MS[c, 1:2, i * E:(i + 1) * E] = jnp.sum(ACC[1, i], axis=0, keepdims=True)
        send(MS.at[c], MS.at[c], "MS", 0, sib)

    def mom1b():
        recv(MS.at[o], "MS", 0)
        MO[z] = MS[0] + MS[1]
        for k in (4, 3, 5, 2, 6, 1, 7):
            send(MO.at[z], MO.at[z], "MO", z, dev(x, y, wrap(z + k, NZ), c))

    def mom2():
        for k in (1, 7, 2, 6, 3, 5, 4):
            recv(MO.at[wrap(z + k, NZ)], "MO", wrap(z + k, NZ))
        for r, dst in ((0, MA.at[y]), (1, MB.at[x])):
            t = MO[0, r:r + 1, :]
            for k in range(1, NZ):
                t = t + MO[k, r:r + 1, :]
            dst[...] = t
        for k in (2, 1, 3):
            send(MA.at[y], MA.at[y], "MA", y, dev(x, wrap(y + k, NY), z, c))
            send(MB.at[x], MB.at[x], "MB", x, dev(wrap(x + k, NX), y, z, c))

    def mom3():
        for k in (1, 3, 2):
            recv(MA.at[wrap(y + k, NY)], "MA", wrap(y + k, NY))
            recv(MB.at[wrap(x + k, NX)], "MB", wrap(x + k, NX))
        FIN[4:5, :] = ((MA[0] + MA[1]) + (MA[2] + MA[3])) * SCALE
        FIN[5:6, :] = ((MB[0] + MB[1]) + (MB[2] + MB[3])) * SCALE

    def part(v, u, first, w):
        h = slice(0, 2) if first else slice(2, 4)
        return PB.at[v, u, w, h] if v == 0 else PB.at[v, u, h, w]

    def ways(v):
        return (y, NY, yp, ym) if v == 0 else (x, NX, xp, xm)

    def bw1(v, u):
        t = None
        for k in range(4):
            if v == 0:
                g = GS[POS[u, k]].reshape(E, E)
                d = lax.dot_general(TB[:, k * E:(k + 1) * E], g, (((1,), (1,)), ((), ())), preferred_element_type=F32)
            else:
                g = GS[POS[k, u]].reshape(E, E)
                d = jnp.dot(TA[:, k * E:(k + 1) * E], g, preferred_element_type=F32)
            t = d if t is None else t + d
        PB[v, u] = (SCALE * t).astype(BF16).reshape(4, 4, R, E)
        pos, n, to_p, to_m = ways(v)
        i = 8 * v + 2 * u
        send(part(v, u, True, wrap(pos + 2, n)), BH.at[v, u, 0], "BH", i, to_p)
        send(part(v, u, False, wrap(pos + 2, n)), BH.at[v, u, 1], "BH", i + 1, to_m)
        send(part(v, u, False, wrap(pos + 1, n)), BF.at[v, u, 0, 2:4], "BF", 2 * i + 1, to_p)
        send(part(v, u, True, wrap(pos - 1, n)), BF.at[v, u, 1, 0:2], "BF", 2 * i + 2, to_m)

    def bw2(v, u):
        pos, n, to_p, to_m = ways(v)
        i = 8 * v + 2 * u
        recv(BH.at[v, u, 0], "BH", i)
        src = part(v, u, True, wrap(pos + 1, n))
        src[...] = (src[...].astype(F32) + BH[v, u, 0].astype(F32)).astype(BF16)
        send(src, BF.at[v, u, 0, 0:2], "BF", 2 * i, to_p)
        recv(BH.at[v, u, 1], "BH", i + 1)
        src = part(v, u, False, wrap(pos - 1, n))
        src[...] = (src[...].astype(F32) + BH[v, u, 1].astype(F32)).astype(BF16)
        send(src, BF.at[v, u, 1, 2:4], "BF", 2 * i + 3, to_m)

    def out(v, u):
        i = 2 * (8 * v + 2 * u)
        for k in range(4):
            recv(BF.at[v, u, k // 2, (k % 2) * 2:(k % 2) * 2 + 2], "BF", i + k)
        w = slice(u * E, (u + 1) * E)
        for r in (2, 1, 3, 0):
            if v == 0:
                t = wrap(x + r, NX)
                mine_ = PB[0, u, y, t]
                norm = TA[rows(slot(t, y)), w]
                m, rs = FIN[4:5, w], FIN[1:2, w]
                dst = ga.at[:, pl.ds(pl.multiple_of(x * W + u * E, E), E)]
                fam, at, to = "OA", 4 * u + x, dev(t, y, z, c)
            else:
                t = wrap(y + r, NY)
                mine_ = PB[1, u, t, x]
                norm = TB[rows(slot(x, t)), w]
                m, rs = FIN[5:6, w], FIN[3:4, w]
                dst = gb.at[:, pl.ds(pl.multiple_of(y * W + u * E, E), E)]
                fam, at, to = "OB", 4 * u + y, dev(x, t, z, c)
            back = mine_.astype(F32) + (BF[v, u, 0, t].astype(F32) + BF[v, u, 1, t].astype(F32))
            grad = (rs * (back - norm.astype(F32) * m)).astype(BF16)
            if r:
                buf = SA if v == 0 else SB
                buf[u, r] = grad
                send(buf.at[u, r], dst, fam, at, to)
            else:
                dst[...] = grad

    ACC[...] = jnp.zeros_like(ACC)
    f1(0)
    st1()
    f1(1)
    f1(2)
    st2()
    f2(0)
    f2(1)
    st3()
    fw(0)
    st4()
    fw(1)
    f2(2)
    st5()
    rest(0)
    comp(0)
    rest(1)
    comp(1)
    comp(2)
    fw(2)
    add(0)
    rs1(0)
    add(1)
    add(2)
    rs1(1)
    rs1(2)
    rest(2)
    comp(3)
    rs2(0)
    comp(4)
    rs2(1)
    add(3)
    rs1(3)
    add(4)
    rs1(4)
    rs2(2)
    fin(0)
    comp(5)
    rs2(3)
    fin(1)
    rs2(4)
    add(5)
    rs1(5)
    fin(2)
    ag1(1)
    fin(3)
    ag1(0)
    fin(4)
    rs2(5)
    ag1(2)
    ag1(3)
    ag2(1)
    ag1(4)
    ag2(0)
    ag2(3)
    fin(5)
    gx(1)
    ag2(4)
    ag2(2)
    gx_wait(1)
    gx(0)
    gx(3)
    ag1(5)
    gx_wait(0)
    gx_wait(3)
    bw1(0, 0)
    bw1(1, 0)
    gx(4)
    gx(2)
    ag2(5)
    mom1()
    mom1b()
    gx_wait(2)
    gx_wait(4)
    bw1(0, 1)
    bw1(1, 1)
    bw2(0, 0)
    bw2(1, 0)
    gx(5)
    gx_wait(5)
    bw1(0, 3)
    bw1(1, 3)
    bw1(1, 2)
    bw1(0, 2)
    mom2()
    bw2(1, 1)
    bw2(0, 1)
    bw2(0, 3)
    bw2(1, 3)
    bw2(0, 2)
    bw2(1, 2)
    mom3()
    out(0, 0)
    out(1, 0)
    out(0, 1)
    out(1, 1)
    out(1, 3)
    out(0, 3)
    out(1, 2)
    out(0, 2)
    for u in range(4):
        for k in (1, 3, 2):
            t = wrap(x + k, NX)
            recv(ga.at[:, pl.ds(pl.multiple_of(t * W + u * E, E), E)], "OA", 4 * u + t)
            t = wrap(y + k, NY)
            recv(gb.at[:, pl.ds(pl.multiple_of(t * W + u * E, E), E)], "OB", 4 * u + t)
    for cp in sent:
        cp.wait_send()


def local(view_a, view_b):
    V = pltpu.VMEM
    scratch = [
        V((R, D), BF16), V((R, D), BF16),
        *[V((16, R, w), BF16) for _ in range(2) for _, w in STEPS],
        V((16 * R, W), BF16), V((16 * R, W), BF16),
        V((4, 2, W), F32), V((4, 2, W), F32),
        V((4, 2, W), F32), V((4, 2, W), F32),
        V((4, 2, W), F32), V((4, 2, W), F32),
        V((2, 4, W), F32), V((8, 4, W), F32), V((6, W), F32),
        V((W, W), BF16),
        V((16, 2, NZ, T, E), F32), V((16, NZ, T, E), F32), V((16, NZ, T, E), F32),
        V((2, 16, T, E), BF16), V((2, 16, T, E), BF16),
        V((16, T, 128), BF16), V((16, T, 128), BF16),
        V((16, T, E), BF16), V((16, T, E), BF16),
        V((2, 16, T, E), BF16), V((2, 16, T, E), BF16),
        V((16, T, 128), BF16), V((16, T, 128), BF16),
        V((16, T, E), BF16), V((16, T, E), BF16),
        V((4, NZ, 1, E), F32), V((4, NZ, 1, E), F32),
        V((16, 2, NZ, T, E), BF16), V((2, 4, T, E), F32),
        V((2, 2, W), F32), V((8, 2, W), F32), V((4, 1, W), F32), V((4, 1, W), F32),
        V((2, 4, 4, 4, R, E), BF16),
        V((2, 4, 2, 2, R, E), BF16), V((2, 4, 2, 4, R, E), BF16),
        V((4, 4, R, E), BF16), V((4, 4, R, E), BF16),
        pltpu.SemaphoreType.DMA((N_SEND,)),
        pltpu.SemaphoreType.DMA((N_RECV,)),
    ]
    out = pltpu.VMEM((R, D), BF16)
    return tuple(pl.pallas_call(
        kernel,
        out_shape=(out, out),
        in_specs=[pl.BlockSpec(memory_space=pl.ANY)] * 2,
        out_specs=(pl.BlockSpec(memory_space=pltpu.VMEM),) * 2,
        scratch_shapes=scratch,
        compiler_params=pltpu.CompilerParams(
            collective_id=0, has_side_effects=True, vmem_limit_bytes=56 * 1024 * 1024),
    )(view_a, view_b))


def solution(mesh):
    spec = P(("dp", "mp"), None)
    return jax.shard_map(local, mesh=mesh, in_specs=(spec, spec), out_specs=(spec, spec), check_vma=False)
```

```python
import jax
import jax.numpy as jnp
from jax import lax
from jax.experimental import pallas as pl
from jax.experimental.pallas import tpu as pltpu
from jax.sharding import PartitionSpec as P

NX, NY, NZ, NC = 4, 4, 8, 2
R = 64
D = 4096
W = 1024
E = 256
T = 16
BLOCKS = ((0, 0), (1, 0), (0, 1), (1, 1), (2, 0), (0, 2), (3, 0), (0, 3), (2, 1),
          (1, 2), (3, 1), (1, 3), (2, 2), (3, 2), (2, 3), (3, 3))
POS = {ij: p for p, ij in enumerate(BLOCKS)}
SETS = ((0, 4), (4, 6), (6, 8), (8, 10), (10, 12), (12, 13), (13, 16))
RECTS = (((0, 2, 0, 2),), ((2, 1, 0, 1), (0, 1, 2, 1)), ((3, 1, 0, 1), (0, 1, 3, 1)), ((2, 1, 1, 1), (1, 1, 2, 1)),
        ((3, 1, 1, 1), (1, 1, 3, 1)), ((2, 1, 2, 1),), ((3, 1, 2, 2), (2, 1, 3, 1)))
SHORT = (2, 3, 5, 6)
STEPS = ((0, 512), (512, 256), (768, 256))
N = 16384
OFF_WEIGHT = 0.0051
EPS = 1e-05
SCALE = 16.0
F32 = jnp.float32
BF16 = jnp.bfloat16
MESH = pl.DeviceIdType.MESH

_SIZES = dict(
    A1=12, B1=12, A2=24, B2=24, S1A=4, S1B=4, S2A=4, S2B=4, SC=1, S3=8, CX=7,
    Z1P=14, Z1M=14, ZHP=7, ZHM=7, Z2P=7, Z2M=7, DV=32, GF=56, GH=14, GX=7, MS=1, MO=8, MA=4, MB=4,
    BH=32, BF=32, OA=16, OB=16, LOC=2,
)
SEM = {}
_n = 0
for _k, _v in _SIZES.items():
    SEM[_k] = _n
    _n += _v
N_RECV = _n
N_SEND = 360


def kernel(a_hbm, b_hbm, ga, gb, a_in, b_in, RA0, RA1, RA2, RB0, RB1, RB2, TA, TB, S0A, S0B, S1A, S1B, S2A, S2B, SC, S3, FIN,
           TT, C2, CR, CO, Z1P, Z1M, ZHP, ZHM, Z2P, Z2M, Y1P, Y1M, YHP, YHM, Y2P, Y2M, DS, DV, GS, ACC, MS, MO, MA, MB,
           PB, BH, BF,
           SA, SB, ssem, rsem):
    me = lax.axis_index("dp")
    c = lax.axis_index("mp")
    x = me // (NZ * NY)
    z = (me // NY) % NZ
    y = me % NY
    o = 1 - c

    def dev(xx, yy, zz, cc):
        return {"dp": xx * (NZ * NY) + zz * NY + yy, "mp": cc}

    def wrap(v, n):
        return (v + n) % n

    peers = [dev(wrap(x + k, NX), y, z, c) for k in range(1, NX)]
    peers += [dev(x, wrap(y + k, NY), z, c) for k in range(1, NY)]
    peers += [dev(x, y, wrap(z + k, NZ), c) for k in range(1, NZ)]
    peers += [dev(x, y, z, 1 - c)]
    barrier = pltpu.get_barrier_semaphore()
    for p in peers:
        pl.semaphore_signal(barrier, inc=1, device_id=p, device_id_type=MESH)
    la = pltpu.make_async_copy(a_hbm, a_in, rsem.at[SEM["LOC"]])
    lb = pltpu.make_async_copy(b_hbm, b_in, rsem.at[SEM["LOC"] + 1])
    la.start()
    lb.start()

    xp, xm = dev(wrap(x + 1, NX), y, z, c), dev(wrap(x - 1, NX), y, z, c)
    yp, ym = dev(x, wrap(y + 1, NY), z, c), dev(x, wrap(y - 1, NY), z, c)
    zp, zm = dev(x, y, wrap(z + 1, NZ), c), dev(x, y, wrap(z - 1, NZ), c)
    sib = dev(x, y, z, o)

    RA, RB = (RA0, RA1, RA2), (RB0, RB1, RB2)
    sent = []

    def send(src, dst, fam, idx, to):
        cp = pltpu.make_async_remote_copy(
            src_ref=src, dst_ref=dst, send_sem=ssem.at[len(sent)], recv_sem=rsem.at[SEM[fam] + idx],
            device_id=to, device_id_type=MESH)
        cp.start()
        sent.append(cp)

    def recv(dst, fam, idx):
        pltpu.make_async_remote_copy(
            src_ref=dst, dst_ref=dst, send_sem=ssem.at[0], recv_sem=rsem.at[SEM[fam] + idx],
            device_id=sib, device_id_type=MESH).wait_recv()

    def cols(i, w=W):
        return pl.ds(pl.multiple_of(i * w, w), w)

    def part_of(i, off, w):
        return pl.ds(pl.multiple_of(i * W + off, w), w)

    def slot(xx, yy):
        return yy * NX + xx

    def rows(s):
        return pl.ds(pl.multiple_of(s * R, R), R)

    def local_stats(v_ref, s_ref):
        for i in range(4):
            v = v_ref[:, i * W:(i + 1) * W].astype(F32)
            m = jnp.sum(v, axis=0, keepdims=True) * (1.0 / R)
            d = v - m
            s_ref[i, 0:1, :] = m
            s_ref[i, 1:2, :] = jnp.sum(d * d, axis=0, keepdims=True)

    la.wait()
    local_stats(a_in, S0A)
    for (off, w), buf in zip(STEPS, RA):
        buf[y * 4 + x] = a_in[:, part_of(x, off, w)]
    lb.wait()
    local_stats(b_in, S0B)
    for (off, w), buf in zip(STEPS, RB):
        buf[x * 4 + y] = b_in[:, part_of(y, off, w)]
    pl.semaphore_wait(barrier, len(peers))

    def f1(n):
        off, w = STEPS[n]
        for k in (2, 1, 3):
            t = wrap(x + k, NX)
            send(a_in.at[:, part_of(t, off, w)], RA[n].at[y * 4 + x], "A1", 4 * n + x, dev(t, y, z, c))
            t = wrap(y + k, NY)
            send(b_in.at[:, part_of(t, off, w)], RB[n].at[x * 4 + y], "B1", 4 * n + y, dev(x, t, z, c))

    def two(buf, w, h):
        return buf.at[pl.ds(pl.multiple_of(w * 4 + 2 * h, 2), 2)]

    def f2(n):
        for k in (1, 3, 2):
            t = wrap(x + k, NX)
            recv(RA[n].at[y * 4 + t], "A1", 4 * n + t)
            t = wrap(y + k, NY)
            recv(RB[n].at[x * 4 + t], "B1", 4 * n + t)
        for h in (0, 1):
            for buf, fam, w, to_p, to_m in ((RA[n], "A2", y, yp, ym), (RB[n], "B2", x, xp, xm)):
                a, b = two(buf, w, h), two(buf, w, 1 - h)
                send(a, a, fam, 8 * n + 2 * w + h, to_p)
                send(b, b, fam, 8 * n + 2 * w + 1 - h, to_m)

    views = (("A2", y, NY, yp, ym), ("B2", x, NX, xp, xm))

    def fw(n):
        for (fam, w, size, to_p, to_m), buf in zip(views, (RA[n], RB[n])):
            for h, t, to in ((0, wrap(w - 1, size), to_p), (1, wrap(w + 1, size), to_m)):
                a = two(buf, t, h)
                recv(a, fam, 8 * n + 2 * t + h)
                send(a, a, fam, 8 * n + 2 * t + h, to)

    def norm(n, ta, tb):
        off, w = STEPS[n]
        cs = slice(off, off + w)

        def body(i, _):
            v = (RA[n][ta * 4 + i].astype(F32) - FIN[0:1, cs]) * FIN[1:2, cs]
            TA[rows(slot(i, ta)), cs] = v.astype(BF16)
            v = (RB[n][tb * 4 + i].astype(F32) - FIN[2:3, cs]) * FIN[3:4, cs]
            TB[rows(slot(tb, i)), cs] = v.astype(BF16)
            return 0

        lax.fori_loop(0, 4, body, 0)
        at = pl.ds(pl.multiple_of(ta * 4 * R, 4 * R), 4 * R)
        TT[cs, at] = TA[at, cs].T

    def rest(n):
        norm(n, y, x)
        for (fam, w, size, _, _), buf in zip(views, (RA[n], RB[n])):
            for h, t in ((1, wrap(w - 1, size)), (0, wrap(w + 1, size))):
                recv(two(buf, t, h), fam, 8 * n + 2 * t + h)
        norm(n, wrap(y - 1, NY), wrap(x - 1, NX))
        norm(n, wrap(y + 1, NY), wrap(x + 1, NX))
        for (fam, w, size, _, _), buf in zip(views, (RA[n], RB[n])):
            t = wrap(w + 2, size)
            for h in (0, 1):
                recv(two(buf, t, h), fam, 8 * n + 2 * t + h)
        norm(n, wrap(y + 2, NY), wrap(x + 2, NX))

    def merge(parts, n):
        mean = parts[0][0]
        for m, _ in parts[1:]:
            mean = mean + m
        mean = mean * (1.0 / len(parts))
        total = None
        for m, q in parts:
            d = m - mean
            t = q + n * (d * d)
            total = t if total is None else total + t
        return mean, total

    def st1():
        for k in (2, 1, 3):
            t = wrap(x + k, NX)
            send(S0A.at[t], S1A.at[x], "S1A", x, dev(t, y, z, c))
            t = wrap(y + k, NY)
            send(S0B.at[t], S1B.at[y], "S1B", y, dev(x, t, z, c))
        S1A[x] = S0A[x]
        S1B[y] = S0B[y]

    def st2():
        for k in (1, 3, 2):
            recv(S1A.at[wrap(x + k, NX)], "S1A", wrap(x + k, NX))
            recv(S1B.at[wrap(y + k, NY)], "S1B", wrap(y + k, NY))
        for src, dst, w in ((S1A, S2A, y), (S1B, S2B, x)):
            mean, m2 = merge([(src[k, 0:1, :], src[k, 1:2, :]) for k in range(4)], float(R))
            dst[w, 0:1, :] = mean
            dst[w, 1:2, :] = m2
        for k in (2, 1, 3):
            send(S2A.at[y], S2A.at[y], "S2A", y, dev(x, wrap(y + k, NY), z, c))
            send(S2B.at[x], S2B.at[x], "S2B", x, dev(wrap(x + k, NX), y, z, c))

    def st3():
        for k in (1, 3, 2):
            recv(S2A.at[wrap(y + k, NY)], "S2A", wrap(y + k, NY))
            recv(S2B.at[wrap(x + k, NX)], "S2B", wrap(x + k, NX))
        for v, src in ((0, S2A), (1, S2B)):
            mean, m2 = merge([(src[k, 0:1, :], src[k, 1:2, :]) for k in range(4)], 4.0 * R)
            SC[c, 2 * v:2 * v + 1, :] = mean
            SC[c, 2 * v + 1:2 * v + 2, :] = m2
        send(SC.at[c], SC.at[c], "SC", 0, sib)

    def st4():
        recv(SC.at[o], "SC", 0)
        for v in (0, 1):
            mean, m2 = merge([(SC[k, 2 * v:2 * v + 1, :], SC[k, 2 * v + 1:2 * v + 2, :]) for k in range(2)], 16.0 * R)
            S3[z, 2 * v:2 * v + 1, :] = mean
            S3[z, 2 * v + 1:2 * v + 2, :] = m2
        for k in (4, 3, 5, 2, 6, 1, 7):
            send(S3.at[z], S3.at[z], "S3", z, dev(x, y, wrap(z + k, NZ), c))

    def st5():
        for k in (1, 7, 2, 6, 3, 5, 4):
            recv(S3.at[wrap(z + k, NZ)], "S3", wrap(z + k, NZ))
        for v in (0, 1):
            mean, m2 = merge([(S3[k, 2 * v:2 * v + 1, :], S3[k, 2 * v + 1:2 * v + 2, :]) for k in range(8)], 32.0 * R)
            FIN[2 * v:2 * v + 1, :] = mean
            FIN[2 * v + 1:2 * v + 2, :] = lax.rsqrt(m2 * (1.0 / N) + EPS)

    def comp(n):
        p0, p1 = SETS[n]
        for i, ni, j, nj in RECTS[n]:
            t = jnp.dot(TT[i * E:(i + ni) * E, :], TB[:, j * E:(j + nj) * E], preferred_element_type=F32)
            for a in range(ni):
                for b in range(nj):
                    C2[POS[i + a, j + b]] = t[a * E:(a + 1) * E, b * E:(b + 1) * E].reshape(2, NZ, T, E)
        send(C2.at[p0:p1, o], CR.at[p0:p1], "CX", n, sib)

    zz = lax.broadcasted_iota(jnp.int32, (T, E), 1) - lax.broadcasted_iota(jnp.int32, (T, E), 0)

    def add(n):
        p0, p1 = SETS[n]
        recv(CR.at[p0:p1], "CX", n)

        def body(p, _):
            CO[p] = C2[p, c] + CR[p]
            return 0

        lax.fori_loop(p0, p1, body, 0)
        for p in range(p0, p1):
            i, j = BLOCKS[p]
            if i == j:
                for q in range(NZ):
                    DS[i, q] = jnp.sum(jnp.where(zz == c * 128 + q * T, CO[p, q], 0.0), axis=0, keepdims=True)

    zp2, zm2 = dev(x, y, wrap(z + 2, NZ), c), dev(x, y, wrap(z - 2, NZ), c)
    q4 = (z + 4) % NZ

    def rs1(n):
        p0, p1 = SETS[n]
        sl = slice(p0, p1)
        v = CO[sl, q4].astype(BF16)
        ZHP[sl] = v[:, :, :128]
        ZHM[sl] = v[:, :, 128:]
        send(ZHP.at[sl], YHP.at[sl], "ZHP", n, zp2)
        send(ZHM.at[sl], YHM.at[sl], "ZHM", n, zm2)
        for k in (1, 0):
            d = 1 + 2 * k
            Z1P[k, sl] = CO[sl, wrap(z + d, NZ)].astype(BF16)
            send(Z1P.at[k, sl], Y1P.at[k, sl], "Z1P", 2 * n + k, zp)
            Z1M[k, sl] = CO[sl, wrap(z - d, NZ)].astype(BF16)
            send(Z1M.at[k, sl], Y1M.at[k, sl], "Z1M", 2 * n + k, zm)
        for p in range(p0, p1):
            i, j = BLOCKS[p]
            if i == j:
                for k in range(1, NZ):
                    q = wrap(z + k, NZ)
                    send(DS.at[i, q], DV.at[i, z], "DV", i * NZ + z, dev(x, y, q, c))
                DV[i, z] = DS[i, z]

    def rs2(n):
        sl = slice(*SETS[n])
        recv(YHP.at[sl], "ZHP", n)
        recv(Y1P.at[1, sl], "Z1P", 2 * n + 1)
        v = CO[sl, wrap(z + 2, NZ)] + Y1P[1, sl].astype(F32)
        h = YHP[sl].astype(F32)
        Z2P[sl] = jnp.concatenate([v[:, :, :128] + h, v[:, :, 128:]], axis=2).astype(BF16)
        send(Z2P.at[sl], Y2P.at[sl], "Z2P", n, zp2)
        recv(YHM.at[sl], "ZHM", n)
        recv(Y1M.at[1, sl], "Z1M", 2 * n + 1)
        v = CO[sl, wrap(z - 2, NZ)] + Y1M[1, sl].astype(F32)
        h = YHM[sl].astype(F32)
        Z2M[sl] = jnp.concatenate([v[:, :, :128], v[:, :, 128:] + h], axis=2).astype(BF16)
        send(Z2M.at[sl], Y2M.at[sl], "Z2M", n, zm2)

    def fin(n):
        p0, p1 = SETS[n]
        sl = slice(p0, p1)
        recv(Y1P.at[0, sl], "Z1P", 2 * n)
        recv(Y1M.at[0, sl], "Z1M", 2 * n)
        recv(Y2P.at[sl], "Z2P", n)
        recv(Y2M.at[sl], "Z2M", n)
        for p in range(p0, p1):
            i, j = BLOCKS[p]
            cc = CO[p, z] + ((Y1P[0, p].astype(F32) + Y1M[0, p].astype(F32)) + (Y2P[p].astype(F32) + Y2M[p].astype(F32)))
            if i == j:
                dv = DV[i, z]
                for k in range(1, NZ):
                    q = wrap(z + k, NZ)
                    recv(DV.at[i, q], "DV", i * NZ + q)
                    dv = dv + DV[i, q]
                on = jnp.logical_and(zz == c * 128 + z * T, x == y)
                cc = jnp.where(on, dv, cc) * (1.0 / N)
                g = jnp.where(on, -2.0 * (1.0 - cc), (2.0 * OFF_WEIGHT) * cc).astype(BF16)
            else:
                cc = cc * (1.0 / N)
                g = ((2.0 * OFF_WEIGHT) * cc).astype(BF16)
            GS[p, c, z] = g
            prod = g.astype(F32) * cc
            ACC[0, i] = ACC[0, i] + prod
            ACC[1, j] = ACC[1, j] + prod
        src = GS.at[sl, c, z]
        ways_ = ((1, zp2), (3, zm2), (0, zp), (2, zm)) if n in SHORT else ((0, zp), (2, zm))
        for k, to in ways_:
            send(src, src, "GF", 8 * n + k, to)

    def ag1(n):
        sl = slice(*SETS[n])
        for k, q, to in ((0, wrap(z - 1, NZ), zp), (2, wrap(z + 1, NZ), zm)):
            src = GS.at[sl, c, q]
            recv(src, "GF", 8 * n + k)
            send(src, src, "GF", 8 * n + k + 1, to)

    lanes_p, lanes_m = slice(0, 128), slice(128, 256)

    def ag2(n):
        sl = slice(*SETS[n])
        for k, q, to, to2, lanes in ((1, wrap(z - 2, NZ), zp, zp2, lanes_p), (3, wrap(z + 2, NZ), zm, zm2, lanes_m)):
            src = GS.at[sl, c, q]
            recv(src, "GF", 8 * n + k)
            half = GS.at[sl, c, q, :, lanes]
            send(half, half, "GH", 2 * n + k // 2, to2)
            send(src, src, "GF", 8 * n + 4 + k, to)

    def gx(n):
        sl = slice(*SETS[n])
        near = ((0, wrap(z - 1, NZ)), (2, wrap(z + 1, NZ))) if n in SHORT else ()
        for k, q in near + ((5, wrap(z - 3, NZ)), (7, wrap(z + 3, NZ))):
            recv(GS.at[sl, c, q], "GF", 8 * n + k)
        recv(GS.at[sl, c, q4, :, lanes_p], "GH", 2 * n)
        recv(GS.at[sl, c, q4, :, lanes_m], "GH", 2 * n + 1)
        send(GS.at[sl, c], GS.at[sl, c], "GX", n, sib)

    def gx_wait(n):
        sl = slice(*SETS[n])
        recv(GS.at[sl, o], "GX", n)

    def mom1():
        for i in range(4):
            r = jnp.sum(ACC[0, i], axis=1, keepdims=True)
            MS[c, 0:1, i * E:(i + 1) * E] = jnp.sum(jnp.where(zz == c * 128 + z * T, r, 0.0), axis=0, keepdims=True)
            MS[c, 1:2, i * E:(i + 1) * E] = jnp.sum(ACC[1, i], axis=0, keepdims=True)
        send(MS.at[c], MS.at[c], "MS", 0, sib)

    def mom1b():
        recv(MS.at[o], "MS", 0)
        MO[z] = MS[0] + MS[1]
        for k in (4, 3, 5, 2, 6, 1, 7):
            send(MO.at[z], MO.at[z], "MO", z, dev(x, y, wrap(z + k, NZ), c))

    def mom2():
        for k in (1, 7, 2, 6, 3, 5, 4):
            recv(MO.at[wrap(z + k, NZ)], "MO", wrap(z + k, NZ))
        for r, dst in ((0, MA.at[y]), (1, MB.at[x])):
            t = MO[0, r:r + 1, :]
            for k in range(1, NZ):
                t = t + MO[k, r:r + 1, :]
            dst[...] = t
        for k in (2, 1, 3):
            send(MA.at[y], MA.at[y], "MA", y, dev(x, wrap(y + k, NY), z, c))
            send(MB.at[x], MB.at[x], "MB", x, dev(wrap(x + k, NX), y, z, c))

    def mom3():
        for k in (1, 3, 2):
            recv(MA.at[wrap(y + k, NY)], "MA", wrap(y + k, NY))
            recv(MB.at[wrap(x + k, NX)], "MB", wrap(x + k, NX))
        FIN[4:5, :] = ((MA[0] + MA[1]) + (MA[2] + MA[3])) * SCALE
        FIN[5:6, :] = ((MB[0] + MB[1]) + (MB[2] + MB[3])) * SCALE

    def part(v, u, first, w):
        h = slice(0, 2) if first else slice(2, 4)
        return PB.at[v, u, w, h] if v == 0 else PB.at[v, u, h, w]

    def ways(v):
        return (y, NY, yp, ym) if v == 0 else (x, NX, xp, xm)

    def bw1(v, u):
        t = None
        for k in range(4):
            if v == 0:
                g = GS[POS[u, k]].reshape(E, E)
                d = lax.dot_general(TB[:, k * E:(k + 1) * E], g, (((1,), (1,)), ((), ())), preferred_element_type=F32)
            else:
                g = GS[POS[k, u]].reshape(E, E)
                d = jnp.dot(TA[:, k * E:(k + 1) * E], g, preferred_element_type=F32)
            t = d if t is None else t + d
        PB[v, u] = (SCALE * t).astype(BF16).reshape(4, 4, R, E)
        pos, n, to_p, to_m = ways(v)
        i = 8 * v + 2 * u
        send(part(v, u, True, wrap(pos + 2, n)), BH.at[v, u, 0], "BH", i, to_p)
        send(part(v, u, False, wrap(pos + 2, n)), BH.at[v, u, 1], "BH", i + 1, to_m)
        send(part(v, u, False, wrap(pos + 1, n)), BF.at[v, u, 0, 2:4], "BF", 2 * i + 1, to_p)
        send(part(v, u, True, wrap(pos - 1, n)), BF.at[v, u, 1, 0:2], "BF", 2 * i + 2, to_m)

    def bw2(v, u):
        pos, n, to_p, to_m = ways(v)
        i = 8 * v + 2 * u
        recv(BH.at[v, u, 0], "BH", i)
        src = part(v, u, True, wrap(pos + 1, n))
        src[...] = (src[...].astype(F32) + BH[v, u, 0].astype(F32)).astype(BF16)
        send(src, BF.at[v, u, 0, 0:2], "BF", 2 * i, to_p)
        recv(BH.at[v, u, 1], "BH", i + 1)
        src = part(v, u, False, wrap(pos - 1, n))
        src[...] = (src[...].astype(F32) + BH[v, u, 1].astype(F32)).astype(BF16)
        send(src, BF.at[v, u, 1, 2:4], "BF", 2 * i + 3, to_m)

    def out(v, u):
        i = 2 * (8 * v + 2 * u)
        for k in range(4):
            recv(BF.at[v, u, k // 2, (k % 2) * 2:(k % 2) * 2 + 2], "BF", i + k)
        w = slice(u * E, (u + 1) * E)
        for r in (2, 1, 3, 0):
            if v == 0:
                t = wrap(x + r, NX)
                mine_ = PB[0, u, y, t]
                norm = TA[rows(slot(t, y)), w]
                m, rs = FIN[4:5, w], FIN[1:2, w]
                dst = ga.at[:, pl.ds(pl.multiple_of(x * W + u * E, E), E)]
                fam, at, to = "OA", 4 * u + x, dev(t, y, z, c)
            else:
                t = wrap(y + r, NY)
                mine_ = PB[1, u, t, x]
                norm = TB[rows(slot(x, t)), w]
                m, rs = FIN[5:6, w], FIN[3:4, w]
                dst = gb.at[:, pl.ds(pl.multiple_of(y * W + u * E, E), E)]
                fam, at, to = "OB", 4 * u + y, dev(x, t, z, c)
            back = mine_.astype(F32) + (BF[v, u, 0, t].astype(F32) + BF[v, u, 1, t].astype(F32))
            grad = (rs * (back - norm.astype(F32) * m)).astype(BF16)
            if r:
                buf = SA if v == 0 else SB
                buf[u, r] = grad
                send(buf.at[u, r], dst, fam, at, to)
            else:
                dst[...] = grad

    ACC[...] = jnp.zeros_like(ACC)
    st1()
    f1(0)
    f1(1)
    st2()
    f1(2)
    f2(0)
    st3()
    st4()
    fw(0)
    f2(1)
    f2(2)
    st5()
    rest(0)
    comp(0)
    fw(1)
    add(0)
    rs1(0)
    fw(2)
    rest(1)
    comp(1)
    rs2(0)
    rest(2)
    comp(2)
    add(1)
    rs1(1)
    comp(3)
    comp(4)
    add(2)
    rs1(2)
    comp(5)
    add(3)
    rs1(3)
    add(4)
    rs1(4)
    rs2(1)
    add(5)
    comp(6)
    rs1(5)
    rs2(2)
    fin(0)
    add(6)
    rs1(6)
    rs2(4)
    rs2(3)
    fin(1)
    ag1(0)
    fin(2)
    rs2(6)
    rs2(5)
    ag1(1)
    fin(4)
    ag2(0)
    fin(3)
    ag2(1)
    ag2(2)
    ag1(4)
    fin(5)
    gx(0)
    fin(6)
    ag2(3)
    gx(1)
    gx_wait(0)
    gx(2)
    ag2(4)
    mom1()
    gx_wait(1)
    gx_wait(2)
    bw1(1, 0)
    ag2(6)
    bw1(0, 0)
    ag2(5)
    gx(3)
    gx(4)
    gx_wait(3)
    mom1b()
    gx_wait(4)
    bw1(0, 1)
    bw2(1, 0)
    gx(6)
    bw1(1, 1)
    gx(5)
    gx_wait(6)
    bw1(0, 3)
    bw1(1, 3)
    gx_wait(5)
    bw1(0, 2)
    bw1(1, 2)
    bw2(0, 0)
    mom2()
    bw2(0, 3)
    bw2(0, 2)
    bw2(1, 3)
    bw2(0, 1)
    bw2(1, 1)
    bw2(1, 2)
    mom3()
    out(1, 0)
    out(0, 0)
    out(0, 3)
    out(1, 3)
    out(0, 2)
    out(1, 1)
    out(1, 2)
    out(0, 1)
    for u in range(4):
        for k in (1, 3, 2):
            t = wrap(x + k, NX)
            recv(ga.at[:, pl.ds(pl.multiple_of(t * W + u * E, E), E)], "OA", 4 * u + t)
            t = wrap(y + k, NY)
            recv(gb.at[:, pl.ds(pl.multiple_of(t * W + u * E, E), E)], "OB", 4 * u + t)
    for cp in sent:
        cp.wait_send()


def local(view_a, view_b):
    V = pltpu.VMEM
    scratch = [
        V((R, D), BF16), V((R, D), BF16),
        *[V((16, R, w), BF16) for _ in range(2) for _, w in STEPS],
        V((16 * R, W), BF16), V((16 * R, W), BF16),
        V((4, 2, W), F32), V((4, 2, W), F32),
        V((4, 2, W), F32), V((4, 2, W), F32),
        V((4, 2, W), F32), V((4, 2, W), F32),
        V((2, 4, W), F32), V((8, 4, W), F32), V((6, W), F32),
        V((W, W), BF16),
        V((16, 2, NZ, T, E), F32), V((16, NZ, T, E), F32), V((16, NZ, T, E), F32),
        V((2, 16, T, E), BF16), V((2, 16, T, E), BF16),
        V((16, T, 128), BF16), V((16, T, 128), BF16),
        V((16, T, E), BF16), V((16, T, E), BF16),
        V((2, 16, T, E), BF16), V((2, 16, T, E), BF16),
        V((16, T, 128), BF16), V((16, T, 128), BF16),
        V((16, T, E), BF16), V((16, T, E), BF16),
        V((4, NZ, 1, E), F32), V((4, NZ, 1, E), F32),
        V((16, 2, NZ, T, E), BF16), V((2, 4, T, E), F32),
        V((2, 2, W), F32), V((8, 2, W), F32), V((4, 1, W), F32), V((4, 1, W), F32),
        V((2, 4, 4, 4, R, E), BF16),
        V((2, 4, 2, 2, R, E), BF16), V((2, 4, 2, 4, R, E), BF16),
        V((4, 4, R, E), BF16), V((4, 4, R, E), BF16),
        pltpu.SemaphoreType.DMA((N_SEND,)),
        pltpu.SemaphoreType.DMA((N_RECV,)),
    ]
    out = pltpu.VMEM((R, D), BF16)
    return tuple(pl.pallas_call(
        kernel,
        out_shape=(out, out),
        in_specs=[pl.BlockSpec(memory_space=pl.ANY)] * 2,
        out_specs=(pl.BlockSpec(memory_space=pltpu.VMEM),) * 2,
        scratch_shapes=scratch,
        compiler_params=pltpu.CompilerParams(
            collective_id=0, has_side_effects=True, vmem_limit_bytes=56 * 1024 * 1024),
    )(view_a, view_b))


def solution(mesh):
    spec = P(("dp", "mp"), None)
    return jax.shard_map(local, mesh=mesh, in_specs=(spec, spec), out_specs=(spec, spec), check_vma=False)
```

```python
import jax
import jax.numpy as jnp
from jax import lax
from jax.experimental import pallas as pl
from jax.experimental.pallas import tpu as pltpu
from jax.sharding import PartitionSpec as P

NX, NY, NZ, NC = 4, 4, 8, 2
R = 64
D = 4096
W = 1024
E = 256
T = 16
BLOCKS = ((0, 0), (1, 0), (0, 1), (1, 1), (2, 0), (0, 2), (3, 0), (0, 3), (2, 1),
          (1, 2), (3, 1), (1, 3), (2, 2), (3, 2), (2, 3), (3, 3))
POS = {ij: p for p, ij in enumerate(BLOCKS)}
SETS = ((0, 4), (4, 6), (6, 8), (8, 10), (10, 12), (12, 13), (13, 16))
RECTS = (((0, 2, 0, 2),), ((2, 1, 0, 1), (0, 1, 2, 1)), ((3, 1, 0, 1), (0, 1, 3, 1)), ((2, 1, 1, 1), (1, 1, 2, 1)),
        ((3, 1, 1, 1), (1, 1, 3, 1)), ((2, 1, 2, 1),), ((3, 1, 2, 2), (2, 1, 3, 1)))
SHORT = (2, 3, 5, 6)
STEPS = ((0, 512), (512, 256), (768, 256))
N = 16384
OFF_WEIGHT = 0.0051
EPS = 1e-05
SCALE = 16.0
F32 = jnp.float32
BF16 = jnp.bfloat16
MESH = pl.DeviceIdType.MESH

_SIZES = dict(
    A1=12, B1=12, A2=24, B2=24, S1A=4, S1B=4, S2A=4, S2B=4, SC=1, S3=8, CX=7,
    Z1P=14, Z1M=14, ZHP=7, ZHM=7, Z2P=7, Z2M=7, DV=32, GF=56, GH=14, GX=7, MS=1, MO=8, MA=4, MB=4,
    BH=32, BF=32, OA=16, OB=16, LOC=2,
)
SEM = {}
_n = 0
for _k, _v in _SIZES.items():
    SEM[_k] = _n
    _n += _v
N_RECV = _n
N_SEND = 360


def kernel(a_hbm, b_hbm, ga, gb, a_in, b_in, RA0, RA1, RA2, RB0, RB1, RB2, TA, TB, S0A, S0B, S1A, S1B, S2A, S2B, SC, S3, FIN,
           TT, C2, CR, CO, Z1P, Z1M, ZHP, ZHM, Z2P, Z2M, Y1P, Y1M, YHP, YHM, Y2P, Y2M, DS, DV, GS, ACC, MS, MO, MA, MB,
           PB, BH, BF,
           SA, SB, ssem, rsem):
    me = lax.axis_index("dp")
    c = lax.axis_index("mp")
    x = me // (NZ * NY)
    z = (me // NY) % NZ
    y = me % NY
    o = 1 - c

    def dev(xx, yy, zz, cc):
        return {"dp": xx * (NZ * NY) + zz * NY + yy, "mp": cc}

    def wrap(v, n):
        return (v + n) % n

    peers = [dev(wrap(x + k, NX), y, z, c) for k in range(1, NX)]
    peers += [dev(x, wrap(y + k, NY), z, c) for k in range(1, NY)]
    peers += [dev(x, y, wrap(z + k, NZ), c) for k in range(1, NZ)]
    peers += [dev(x, y, z, 1 - c)]
    barrier = pltpu.get_barrier_semaphore()
    for p in peers:
        pl.semaphore_signal(barrier, inc=1, device_id=p, device_id_type=MESH)
    la = pltpu.make_async_copy(a_hbm, a_in, rsem.at[SEM["LOC"]])
    lb = pltpu.make_async_copy(b_hbm, b_in, rsem.at[SEM["LOC"] + 1])
    la.start()
    lb.start()

    xp, xm = dev(wrap(x + 1, NX), y, z, c), dev(wrap(x - 1, NX), y, z, c)
    yp, ym = dev(x, wrap(y + 1, NY), z, c), dev(x, wrap(y - 1, NY), z, c)
    zp, zm = dev(x, y, wrap(z + 1, NZ), c), dev(x, y, wrap(z - 1, NZ), c)
    sib = dev(x, y, z, o)

    RA, RB = (RA0, RA1, RA2), (RB0, RB1, RB2)
    sent = []

    def send(src, dst, fam, idx, to):
        cp = pltpu.make_async_remote_copy(
            src_ref=src, dst_ref=dst, send_sem=ssem.at[len(sent)], recv_sem=rsem.at[SEM[fam] + idx],
            device_id=to, device_id_type=MESH)
        cp.start()
        sent.append(cp)

    def recv(dst, fam, idx):
        pltpu.make_async_remote_copy(
            src_ref=dst, dst_ref=dst, send_sem=ssem.at[0], recv_sem=rsem.at[SEM[fam] + idx],
            device_id=sib, device_id_type=MESH).wait_recv()

    def cols(i, w=W):
        return pl.ds(pl.multiple_of(i * w, w), w)

    def part_of(i, off, w):
        return pl.ds(pl.multiple_of(i * W + off, w), w)

    def slot(xx, yy):
        return yy * NX + xx

    def rows(s):
        return pl.ds(pl.multiple_of(s * R, R), R)

    def local_stats(v_ref, s_ref):
        for i in range(4):
            v = v_ref[:, i * W:(i + 1) * W].astype(F32)
            m = jnp.sum(v, axis=0, keepdims=True) * (1.0 / R)
            d = v - m
            s_ref[i, 0:1, :] = m
            s_ref[i, 1:2, :] = jnp.sum(d * d, axis=0, keepdims=True)

    la.wait()
    local_stats(a_in, S0A)
    for (off, w), buf in zip(STEPS, RA):
        buf[y * 4 + x] = a_in[:, part_of(x, off, w)]
    lb.wait()
    local_stats(b_in, S0B)
    for (off, w), buf in zip(STEPS, RB):
        buf[x * 4 + y] = b_in[:, part_of(y, off, w)]
    pl.semaphore_wait(barrier, len(peers))

    def f1(n):
        off, w = STEPS[n]
        for k in (2, 1, 3):
            t = wrap(x + k, NX)
            send(a_in.at[:, part_of(t, off, w)], RA[n].at[y * 4 + x], "A1", 4 * n + x, dev(t, y, z, c))
            t = wrap(y + k, NY)
            send(b_in.at[:, part_of(t, off, w)], RB[n].at[x * 4 + y], "B1", 4 * n + y, dev(x, t, z, c))

    def two(buf, w, h):
        return buf.at[pl.ds(pl.multiple_of(w * 4 + 2 * h, 2), 2)]

    def f2(n):
        for k in (1, 3, 2):
            t = wrap(x + k, NX)
            recv(RA[n].at[y * 4 + t], "A1", 4 * n + t)
            t = wrap(y + k, NY)
            recv(RB[n].at[x * 4 + t], "B1", 4 * n + t)
        for h in (0, 1):
            for buf, fam, w, to_p, to_m in ((RA[n], "A2", y, yp, ym), (RB[n], "B2", x, xp, xm)):
                a, b = two(buf, w, h), two(buf, w, 1 - h)
                send(a, a, fam, 8 * n + 2 * w + h, to_p)
                send(b, b, fam, 8 * n + 2 * w + 1 - h, to_m)

    views = (("A2", y, NY, yp, ym), ("B2", x, NX, xp, xm))

    def fw(n):
        for (fam, w, size, to_p, to_m), buf in zip(views, (RA[n], RB[n])):
            for h, t, to in ((0, wrap(w - 1, size), to_p), (1, wrap(w + 1, size), to_m)):
                a = two(buf, t, h)
                recv(a, fam, 8 * n + 2 * t + h)
                send(a, a, fam, 8 * n + 2 * t + h, to)

    def norm(n, ta, tb):
        off, w = STEPS[n]
        cs = slice(off, off + w)

        def body(i, _):
            v = (RA[n][ta * 4 + i].astype(F32) - FIN[0:1, cs]) * FIN[1:2, cs]
            TA[rows(slot(i, ta)), cs] = v.astype(BF16)
            v = (RB[n][tb * 4 + i].astype(F32) - FIN[2:3, cs]) * FIN[3:4, cs]
            TB[rows(slot(tb, i)), cs] = v.astype(BF16)
            return 0

        lax.fori_loop(0, 4, body, 0)
        at = pl.ds(pl.multiple_of(ta * 4 * R, 4 * R), 4 * R)
        TT[cs, at] = TA[at, cs].T

    def rest(n):
        norm(n, y, x)
        for (fam, w, size, _, _), buf in zip(views, (RA[n], RB[n])):
            for h, t in ((1, wrap(w - 1, size)), (0, wrap(w + 1, size))):
                recv(two(buf, t, h), fam, 8 * n + 2 * t + h)
        norm(n, wrap(y - 1, NY), wrap(x - 1, NX))
        norm(n, wrap(y + 1, NY), wrap(x + 1, NX))
        for (fam, w, size, _, _), buf in zip(views, (RA[n], RB[n])):
            t = wrap(w + 2, size)
            for h in (0, 1):
                recv(two(buf, t, h), fam, 8 * n + 2 * t + h)
        norm(n, wrap(y + 2, NY), wrap(x + 2, NX))

    def merge(parts, n):
        mean = parts[0][0]
        for m, _ in parts[1:]:
            mean = mean + m
        mean = mean * (1.0 / len(parts))
        total = None
        for m, q in parts:
            d = m - mean
            t = q + n * (d * d)
            total = t if total is None else total + t
        return mean, total

    def st1():
        for k in (2, 1, 3):
            t = wrap(x + k, NX)
            send(S0A.at[t], S1A.at[x], "S1A", x, dev(t, y, z, c))
            t = wrap(y + k, NY)
            send(S0B.at[t], S1B.at[y], "S1B", y, dev(x, t, z, c))
        S1A[x] = S0A[x]
        S1B[y] = S0B[y]

    def st2():
        for k in (1, 3, 2):
            recv(S1A.at[wrap(x + k, NX)], "S1A", wrap(x + k, NX))
            recv(S1B.at[wrap(y + k, NY)], "S1B", wrap(y + k, NY))
        for src, dst, w in ((S1A, S2A, y), (S1B, S2B, x)):
            mean, m2 = merge([(src[k, 0:1, :], src[k, 1:2, :]) for k in range(4)], float(R))
            dst[w, 0:1, :] = mean
            dst[w, 1:2, :] = m2
        for k in (2, 1, 3):
            send(S2A.at[y], S2A.at[y], "S2A", y, dev(x, wrap(y + k, NY), z, c))
            send(S2B.at[x], S2B.at[x], "S2B", x, dev(wrap(x + k, NX), y, z, c))

    def st3():
        for k in (1, 3, 2):
            recv(S2A.at[wrap(y + k, NY)], "S2A", wrap(y + k, NY))
            recv(S2B.at[wrap(x + k, NX)], "S2B", wrap(x + k, NX))
        for v, src in ((0, S2A), (1, S2B)):
            mean, m2 = merge([(src[k, 0:1, :], src[k, 1:2, :]) for k in range(4)], 4.0 * R)
            SC[c, 2 * v:2 * v + 1, :] = mean
            SC[c, 2 * v + 1:2 * v + 2, :] = m2
        send(SC.at[c], SC.at[c], "SC", 0, sib)

    def st4():
        recv(SC.at[o], "SC", 0)
        for v in (0, 1):
            mean, m2 = merge([(SC[k, 2 * v:2 * v + 1, :], SC[k, 2 * v + 1:2 * v + 2, :]) for k in range(2)], 16.0 * R)
            S3[z, 2 * v:2 * v + 1, :] = mean
            S3[z, 2 * v + 1:2 * v + 2, :] = m2
        for k in (4, 3, 5, 2, 6, 1, 7):
            send(S3.at[z], S3.at[z], "S3", z, dev(x, y, wrap(z + k, NZ), c))

    def st5():
        for k in (1, 7, 2, 6, 3, 5, 4):
            recv(S3.at[wrap(z + k, NZ)], "S3", wrap(z + k, NZ))
        for v in (0, 1):
            mean, m2 = merge([(S3[k, 2 * v:2 * v + 1, :], S3[k, 2 * v + 1:2 * v + 2, :]) for k in range(8)], 32.0 * R)
            FIN[2 * v:2 * v + 1, :] = mean
            FIN[2 * v + 1:2 * v + 2, :] = lax.rsqrt(m2 * (1.0 / N) + EPS)

    def comp(n):
        p0, p1 = SETS[n]
        for i, ni, j, nj in RECTS[n]:
            t = jnp.dot(TT[i * E:(i + ni) * E, :], TB[:, j * E:(j + nj) * E], preferred_element_type=F32)
            for a in range(ni):
                for b in range(nj):
                    C2[POS[i + a, j + b]] = t[a * E:(a + 1) * E, b * E:(b + 1) * E].reshape(2, NZ, T, E)
        send(C2.at[p0:p1, o], CR.at[p0:p1], "CX", n, sib)

    zz = lax.broadcasted_iota(jnp.int32, (T, E), 1) - lax.broadcasted_iota(jnp.int32, (T, E), 0)

    def add(n):
        p0, p1 = SETS[n]
        recv(CR.at[p0:p1], "CX", n)

        def body(p, _):
            CO[p] = C2[p, c] + CR[p]
            return 0

        lax.fori_loop(p0, p1, body, 0)
        for p in range(p0, p1):
            i, j = BLOCKS[p]
            if i == j:
                for q in range(NZ):
                    DS[i, q] = jnp.sum(jnp.where(zz == c * 128 + q * T, CO[p, q], 0.0), axis=0, keepdims=True)

    zp2, zm2 = dev(x, y, wrap(z + 2, NZ), c), dev(x, y, wrap(z - 2, NZ), c)
    q4 = (z + 4) % NZ

    def rs1(n):
        p0, p1 = SETS[n]
        sl = slice(p0, p1)
        v = CO[sl, q4].astype(BF16)
        ZHP[sl] = v[:, :, :128]
        ZHM[sl] = v[:, :, 128:]
        send(ZHP.at[sl], YHP.at[sl], "ZHP", n, zp2)
        send(ZHM.at[sl], YHM.at[sl], "ZHM", n, zm2)
        for k in (1, 0):
            d = 1 + 2 * k
            Z1P[k, sl] = CO[sl, wrap(z + d, NZ)].astype(BF16)
            send(Z1P.at[k, sl], Y1P.at[k, sl], "Z1P", 2 * n + k, zp)
            Z1M[k, sl] = CO[sl, wrap(z - d, NZ)].astype(BF16)
            send(Z1M.at[k, sl], Y1M.at[k, sl], "Z1M", 2 * n + k, zm)
        for p in range(p0, p1):
            i, j = BLOCKS[p]
            if i == j:
                for k in range(1, NZ):
                    q = wrap(z + k, NZ)
                    send(DS.at[i, q], DV.at[i, z], "DV", i * NZ + z, dev(x, y, q, c))
                DV[i, z] = DS[i, z]

    def rs2(n):
        sl = slice(*SETS[n])
        recv(YHP.at[sl], "ZHP", n)
        recv(Y1P.at[1, sl], "Z1P", 2 * n + 1)
        v = CO[sl, wrap(z + 2, NZ)] + Y1P[1, sl].astype(F32)
        h = YHP[sl].astype(F32)
        Z2P[sl] = jnp.concatenate([v[:, :, :128] + h, v[:, :, 128:]], axis=2).astype(BF16)
        send(Z2P.at[sl], Y2P.at[sl], "Z2P", n, zp2)
        recv(YHM.at[sl], "ZHM", n)
        recv(Y1M.at[1, sl], "Z1M", 2 * n + 1)
        v = CO[sl, wrap(z - 2, NZ)] + Y1M[1, sl].astype(F32)
        h = YHM[sl].astype(F32)
        Z2M[sl] = jnp.concatenate([v[:, :, :128], v[:, :, 128:] + h], axis=2).astype(BF16)
        send(Z2M.at[sl], Y2M.at[sl], "Z2M", n, zm2)

    def fin(n):
        p0, p1 = SETS[n]
        sl = slice(p0, p1)
        recv(Y1P.at[0, sl], "Z1P", 2 * n)
        recv(Y1M.at[0, sl], "Z1M", 2 * n)
        recv(Y2P.at[sl], "Z2P", n)
        recv(Y2M.at[sl], "Z2M", n)
        for p in range(p0, p1):
            i, j = BLOCKS[p]
            cc = CO[p, z] + ((Y1P[0, p].astype(F32) + Y1M[0, p].astype(F32)) + (Y2P[p].astype(F32) + Y2M[p].astype(F32)))
            if i == j:
                dv = DV[i, z]
                for k in range(1, NZ):
                    q = wrap(z + k, NZ)
                    recv(DV.at[i, q], "DV", i * NZ + q)
                    dv = dv + DV[i, q]
                on = jnp.logical_and(zz == c * 128 + z * T, x == y)
                cc = jnp.where(on, dv, cc) * (1.0 / N)
                g = jnp.where(on, -2.0 * (1.0 - cc), (2.0 * OFF_WEIGHT) * cc).astype(BF16)
            else:
                cc = cc * (1.0 / N)
                g = ((2.0 * OFF_WEIGHT) * cc).astype(BF16)
            GS[p, c, z] = g
            prod = g.astype(F32) * cc
            ACC[0, i] = ACC[0, i] + prod
            ACC[1, j] = ACC[1, j] + prod
        src = GS.at[sl, c, z]
        ways_ = ((1, zp2), (3, zm2), (0, zp), (2, zm)) if n in SHORT else ((0, zp), (2, zm))
        for k, to in ways_:
            send(src, src, "GF", 8 * n + k, to)

    def ag1(n):
        sl = slice(*SETS[n])
        for k, q, to in ((0, wrap(z - 1, NZ), zp), (2, wrap(z + 1, NZ), zm)):
            src = GS.at[sl, c, q]
            recv(src, "GF", 8 * n + k)
            send(src, src, "GF", 8 * n + k + 1, to)

    lanes_p, lanes_m = slice(0, 128), slice(128, 256)

    def ag2(n):
        sl = slice(*SETS[n])
        for k, q, to, to2, lanes in ((1, wrap(z - 2, NZ), zp, zp2, lanes_p), (3, wrap(z + 2, NZ), zm, zm2, lanes_m)):
            src = GS.at[sl, c, q]
            recv(src, "GF", 8 * n + k)
            half = GS.at[sl, c, q, :, lanes]
            send(half, half, "GH", 2 * n + k // 2, to2)
            send(src, src, "GF", 8 * n + 4 + k, to)

    def gx(n):
        sl = slice(*SETS[n])
        near = ((0, wrap(z - 1, NZ)), (2, wrap(z + 1, NZ))) if n in SHORT else ()
        for k, q in near + ((5, wrap(z - 3, NZ)), (7, wrap(z + 3, NZ))):
            recv(GS.at[sl, c, q], "GF", 8 * n + k)
        recv(GS.at[sl, c, q4, :, lanes_p], "GH", 2 * n)
        recv(GS.at[sl, c, q4, :, lanes_m], "GH", 2 * n + 1)
        send(GS.at[sl, c], GS.at[sl, c], "GX", n, sib)

    def gx_wait(n):
        sl = slice(*SETS[n])
        recv(GS.at[sl, o], "GX", n)

    def mom1():
        for i in range(4):
            r = jnp.sum(ACC[0, i], axis=1, keepdims=True)
            MS[c, 0:1, i * E:(i + 1) * E] = jnp.sum(jnp.where(zz == c * 128 + z * T, r, 0.0), axis=0, keepdims=True)
            MS[c, 1:2, i * E:(i + 1) * E] = jnp.sum(ACC[1, i], axis=0, keepdims=True)
        send(MS.at[c], MS.at[c], "MS", 0, sib)

    def mom1b():
        recv(MS.at[o], "MS", 0)
        MO[z] = MS[0] + MS[1]
        for k in (4, 3, 5, 2, 6, 1, 7):
            send(MO.at[z], MO.at[z], "MO", z, dev(x, y, wrap(z + k, NZ), c))

    def mom2():
        for k in (1, 7, 2, 6, 3, 5, 4):
            recv(MO.at[wrap(z + k, NZ)], "MO", wrap(z + k, NZ))
        for r, dst in ((0, MA.at[y]), (1, MB.at[x])):
            t = MO[0, r:r + 1, :]
            for k in range(1, NZ):
                t = t + MO[k, r:r + 1, :]
            dst[...] = t
        for k in (2, 1, 3):
            send(MA.at[y], MA.at[y], "MA", y, dev(x, wrap(y + k, NY), z, c))
            send(MB.at[x], MB.at[x], "MB", x, dev(wrap(x + k, NX), y, z, c))

    def mom3():
        for k in (1, 3, 2):
            recv(MA.at[wrap(y + k, NY)], "MA", wrap(y + k, NY))
            recv(MB.at[wrap(x + k, NX)], "MB", wrap(x + k, NX))
        FIN[4:5, :] = ((MA[0] + MA[1]) + (MA[2] + MA[3])) * SCALE
        FIN[5:6, :] = ((MB[0] + MB[1]) + (MB[2] + MB[3])) * SCALE

    def part(v, u, first, w):
        h = slice(0, 2) if first else slice(2, 4)
        return PB.at[v, u, w, h] if v == 0 else PB.at[v, u, h, w]

    def ways(v):
        return (y, NY, yp, ym) if v == 0 else (x, NX, xp, xm)

    def bw1(v, u):
        t = None
        for k in range(4):
            if v == 0:
                g = GS[POS[u, k]].reshape(E, E)
                d = lax.dot_general(TB[:, k * E:(k + 1) * E], g, (((1,), (1,)), ((), ())), preferred_element_type=F32)
            else:
                g = GS[POS[k, u]].reshape(E, E)
                d = jnp.dot(TA[:, k * E:(k + 1) * E], g, preferred_element_type=F32)
            t = d if t is None else t + d
        PB[v, u] = (SCALE * t).astype(BF16).reshape(4, 4, R, E)
        pos, n, to_p, to_m = ways(v)
        i = 8 * v + 2 * u
        send(part(v, u, True, wrap(pos + 2, n)), BH.at[v, u, 0], "BH", i, to_p)
        send(part(v, u, False, wrap(pos + 2, n)), BH.at[v, u, 1], "BH", i + 1, to_m)
        send(part(v, u, False, wrap(pos + 1, n)), BF.at[v, u, 0, 2:4], "BF", 2 * i + 1, to_p)
        send(part(v, u, True, wrap(pos - 1, n)), BF.at[v, u, 1, 0:2], "BF", 2 * i + 2, to_m)

    def bw2(v, u):
        pos, n, to_p, to_m = ways(v)
        i = 8 * v + 2 * u
        recv(BH.at[v, u, 0], "BH", i)
        src = part(v, u, True, wrap(pos + 1, n))
        src[...] = (src[...].astype(F32) + BH[v, u, 0].astype(F32)).astype(BF16)
        send(src, BF.at[v, u, 0, 0:2], "BF", 2 * i, to_p)
        recv(BH.at[v, u, 1], "BH", i + 1)
        src = part(v, u, False, wrap(pos - 1, n))
        src[...] = (src[...].astype(F32) + BH[v, u, 1].astype(F32)).astype(BF16)
        send(src, BF.at[v, u, 1, 2:4], "BF", 2 * i + 3, to_m)

    def out(v, u):
        i = 2 * (8 * v + 2 * u)
        for k in range(4):
            recv(BF.at[v, u, k // 2, (k % 2) * 2:(k % 2) * 2 + 2], "BF", i + k)
        w = slice(u * E, (u + 1) * E)
        for r in (2, 1, 3, 0):
            if v == 0:
                t = wrap(x + r, NX)
                mine_ = PB[0, u, y, t]
                norm = TA[rows(slot(t, y)), w]
                m, rs = FIN[4:5, w], FIN[1:2, w]
                dst = ga.at[:, pl.ds(pl.multiple_of(x * W + u * E, E), E)]
                fam, at, to = "OA", 4 * u + x, dev(t, y, z, c)
            else:
                t = wrap(y + r, NY)
                mine_ = PB[1, u, t, x]
                norm = TB[rows(slot(x, t)), w]
                m, rs = FIN[5:6, w], FIN[3:4, w]
                dst = gb.at[:, pl.ds(pl.multiple_of(y * W + u * E, E), E)]
                fam, at, to = "OB", 4 * u + y, dev(x, t, z, c)
            back = mine_.astype(F32) + (BF[v, u, 0, t].astype(F32) + BF[v, u, 1, t].astype(F32))
            grad = (rs * (back - norm.astype(F32) * m)).astype(BF16)
            if r:
                buf = SA if v == 0 else SB
                buf[u, r] = grad
                send(buf.at[u, r], dst, fam, at, to)
            else:
                dst[...] = grad

    ACC[...] = jnp.zeros_like(ACC)
    st1()
    f1(0)
    f1(1)
    f1(2)
    st2()
    f2(0)
    st3()
    st4()
    fw(0)
    f2(1)
    f2(2)
    st5()
    rest(0)
    comp(0)
    fw(1)
    add(0)
    rs1(0)
    fw(2)
    rest(1)
    comp(1)
    rs2(0)
    rest(2)
    comp(2)
    add(1)
    rs1(1)
    comp(3)
    comp(4)
    add(2)
    rs1(2)
    comp(5)
    add(3)
    rs1(3)
    add(4)
    rs1(4)
    rs2(1)
    add(5)
    comp(6)
    rs1(5)
    rs2(2)
    fin(0)
    add(6)
    rs1(6)
    rs2(4)
    rs2(3)
    fin(1)
    ag1(0)
    fin(2)
    rs2(6)
    rs2(5)
    ag1(1)
    fin(4)
    ag2(0)
    fin(3)
    ag2(1)
    ag2(2)
    ag1(4)
    fin(5)
    gx(0)
    fin(6)
    ag2(3)
    gx(1)
    gx_wait(0)
    gx(2)
    ag2(4)
    mom1()
    gx_wait(1)
    gx_wait(2)
    bw1(1, 0)
    ag2(6)
    bw1(0, 0)
    ag2(5)
    gx(3)
    gx(4)
    gx_wait(3)
    mom1b()
    gx_wait(4)
    bw1(0, 1)
    bw2(1, 0)
    gx(6)
    bw1(1, 1)
    gx(5)
    gx_wait(6)
    bw1(0, 3)
    bw1(1, 3)
    gx_wait(5)
    bw1(0, 2)
    bw1(1, 2)
    bw2(0, 0)
    mom2()
    bw2(0, 3)
    bw2(0, 2)
    bw2(0, 1)
    bw2(1, 1)
    bw2(1, 3)
    bw2(1, 2)
    mom3()
    out(1, 0)
    out(0, 0)
    out(0, 3)
    out(1, 3)
    out(0, 2)
    out(1, 1)
    out(1, 2)
    out(0, 1)
    for u in range(4):
        for k in (1, 3, 2):
            t = wrap(x + k, NX)
            recv(ga.at[:, pl.ds(pl.multiple_of(t * W + u * E, E), E)], "OA", 4 * u + t)
            t = wrap(y + k, NY)
            recv(gb.at[:, pl.ds(pl.multiple_of(t * W + u * E, E), E)], "OB", 4 * u + t)
    for cp in sent:
        cp.wait_send()


def local(view_a, view_b):
    V = pltpu.VMEM
    scratch = [
        V((R, D), BF16), V((R, D), BF16),
        *[V((16, R, w), BF16) for _ in range(2) for _, w in STEPS],
        V((16 * R, W), BF16), V((16 * R, W), BF16),
        V((4, 2, W), F32), V((4, 2, W), F32),
        V((4, 2, W), F32), V((4, 2, W), F32),
        V((4, 2, W), F32), V((4, 2, W), F32),
        V((2, 4, W), F32), V((8, 4, W), F32), V((6, W), F32),
        V((W, W), BF16),
        V((16, 2, NZ, T, E), F32), V((16, NZ, T, E), F32), V((16, NZ, T, E), F32),
        V((2, 16, T, E), BF16), V((2, 16, T, E), BF16),
        V((16, T, 128), BF16), V((16, T, 128), BF16),
        V((16, T, E), BF16), V((16, T, E), BF16),
        V((2, 16, T, E), BF16), V((2, 16, T, E), BF16),
        V((16, T, 128), BF16), V((16, T, 128), BF16),
        V((16, T, E), BF16), V((16, T, E), BF16),
        V((4, NZ, 1, E), F32), V((4, NZ, 1, E), F32),
        V((16, 2, NZ, T, E), BF16), V((2, 4, T, E), F32),
        V((2, 2, W), F32), V((8, 2, W), F32), V((4, 1, W), F32), V((4, 1, W), F32),
        V((2, 4, 4, 4, R, E), BF16),
        V((2, 4, 2, 2, R, E), BF16), V((2, 4, 2, 4, R, E), BF16),
        V((4, 4, R, E), BF16), V((4, 4, R, E), BF16),
        pltpu.SemaphoreType.DMA((N_SEND,)),
        pltpu.SemaphoreType.DMA((N_RECV,)),
    ]
    out = pltpu.VMEM((R, D), BF16)
    return tuple(pl.pallas_call(
        kernel,
        out_shape=(out, out),
        in_specs=[pl.BlockSpec(memory_space=pl.ANY)] * 2,
        out_specs=(pl.BlockSpec(memory_space=pltpu.VMEM),) * 2,
        scratch_shapes=scratch,
        compiler_params=pltpu.CompilerParams(
            collective_id=0, has_side_effects=True, vmem_limit_bytes=56 * 1024 * 1024),
    )(view_a, view_b))


def solution(mesh):
    spec = P(("dp", "mp"), None)
    return jax.shard_map(local, mesh=mesh, in_specs=(spec, spec), out_specs=(spec, spec), check_vma=False)
```

```python
import jax
import jax.numpy as jnp
from jax import lax
from jax.experimental import pallas as pl
from jax.experimental.pallas import tpu as pltpu
from jax.sharding import PartitionSpec as P

NX, NY, NZ, NC = 4, 4, 8, 2
R = 64
D = 4096
W = 1024
E = 256
T = 16
BLOCKS = ((0, 0), (1, 0), (0, 1), (1, 1), (2, 0), (0, 2), (3, 0), (0, 3), (2, 1),
          (1, 2), (3, 1), (1, 3), (2, 2), (3, 2), (2, 3), (3, 3))
POS = {ij: p for p, ij in enumerate(BLOCKS)}
SETS = ((0, 4), (4, 6), (6, 8), (8, 10), (10, 12), (12, 13), (13, 16))
RECTS = (((0, 2, 0, 2),), ((2, 1, 0, 1), (0, 1, 2, 1)), ((3, 1, 0, 1), (0, 1, 3, 1)), ((2, 1, 1, 1), (1, 1, 2, 1)),
        ((3, 1, 1, 1), (1, 1, 3, 1)), ((2, 1, 2, 1),), ((3, 1, 2, 2), (2, 1, 3, 1)))
SHORT = (2, 3, 5, 6)
STEPS = ((0, 512), (512, 256), (768, 256))
N = 16384
OFF_WEIGHT = 0.0051
EPS = 1e-05
SCALE = 16.0
F32 = jnp.float32
BF16 = jnp.bfloat16
MESH = pl.DeviceIdType.MESH

_SIZES = dict(
    A1=12, B1=12, A2=24, B2=24, S1A=4, S1B=4, S2A=4, S2B=4, SC=1, S3=8, CX=7,
    Z1P=14, Z1M=14, ZHP=7, ZHM=7, Z2P=7, Z2M=7, DV=32, GF=56, GH=14, GX=7, MS=1, MO=8, MA=4, MB=4,
    BH=32, BF=32, OA=16, OB=16, LOC=2,
)
SEM = {}
_n = 0
for _k, _v in _SIZES.items():
    SEM[_k] = _n
    _n += _v
N_RECV = _n
N_SEND = 360


def kernel(a_hbm, b_hbm, ga, gb, a_in, b_in, RA0, RA1, RA2, RB0, RB1, RB2, TA, TB, S0A, S0B, S1A, S1B, S2A, S2B, SC, S3, FIN,
           TT, C2, CR, CO, Z1P, Z1M, ZHP, ZHM, Z2P, Z2M, Y1P, Y1M, YHP, YHM, Y2P, Y2M, DS, DV, GS, ACC, MS, MO, MA, MB,
           PB, BH, BF,
           SA, SB, ssem, rsem):
    me = lax.axis_index("dp")
    c = lax.axis_index("mp")
    x = me // (NZ * NY)
    z = (me // NY) % NZ
    y = me % NY
    o = 1 - c

    def dev(xx, yy, zz, cc):
        return {"dp": xx * (NZ * NY) + zz * NY + yy, "mp": cc}

    def wrap(v, n):
        return (v + n) % n

    peers = [dev(wrap(x + k, NX), y, z, c) for k in range(1, NX)]
    peers += [dev(x, wrap(y + k, NY), z, c) for k in range(1, NY)]
    peers += [dev(x, y, wrap(z + k, NZ), c) for k in range(1, NZ)]
    peers += [dev(x, y, z, 1 - c)]
    barrier = pltpu.get_barrier_semaphore()
    for p in peers:
        pl.semaphore_signal(barrier, inc=1, device_id=p, device_id_type=MESH)
    la = pltpu.make_async_copy(a_hbm, a_in, rsem.at[SEM["LOC"]])
    lb = pltpu.make_async_copy(b_hbm, b_in, rsem.at[SEM["LOC"] + 1])
    la.start()
    lb.start()

    xp, xm = dev(wrap(x + 1, NX), y, z, c), dev(wrap(x - 1, NX), y, z, c)
    yp, ym = dev(x, wrap(y + 1, NY), z, c), dev(x, wrap(y - 1, NY), z, c)
    zp, zm = dev(x, y, wrap(z + 1, NZ), c), dev(x, y, wrap(z - 1, NZ), c)
    sib = dev(x, y, z, o)

    RA, RB = (RA0, RA1, RA2), (RB0, RB1, RB2)
    sent = []

    def send(src, dst, fam, idx, to):
        cp = pltpu.make_async_remote_copy(
            src_ref=src, dst_ref=dst, send_sem=ssem.at[len(sent)], recv_sem=rsem.at[SEM[fam] + idx],
            device_id=to, device_id_type=MESH)
        cp.start()
        sent.append(cp)

    def recv(dst, fam, idx):
        pltpu.make_async_remote_copy(
            src_ref=dst, dst_ref=dst, send_sem=ssem.at[0], recv_sem=rsem.at[SEM[fam] + idx],
            device_id=sib, device_id_type=MESH).wait_recv()

    def cols(i, w=W):
        return pl.ds(pl.multiple_of(i * w, w), w)

    def part_of(i, off, w):
        return pl.ds(pl.multiple_of(i * W + off, w), w)

    def slot(xx, yy):
        return yy * NX + xx

    def rows(s):
        return pl.ds(pl.multiple_of(s * R, R), R)

    def local_stats(v_ref, s_ref):
        for i in range(4):
            v = v_ref[:, i * W:(i + 1) * W].astype(F32)
            m = jnp.sum(v, axis=0, keepdims=True) * (1.0 / R)
            d = v - m
            s_ref[i, 0:1, :] = m
            s_ref[i, 1:2, :] = jnp.sum(d * d, axis=0, keepdims=True)

    la.wait()
    local_stats(a_in, S0A)
    for (off, w), buf in zip(STEPS, RA):
        buf[y * 4 + x] = a_in[:, part_of(x, off, w)]
    lb.wait()
    local_stats(b_in, S0B)
    for (off, w), buf in zip(STEPS, RB):
        buf[x * 4 + y] = b_in[:, part_of(y, off, w)]
    pl.semaphore_wait(barrier, len(peers))

    def f1(n):
        off, w = STEPS[n]
        for k in (2, 1, 3):
            t = wrap(x + k, NX)
            send(a_in.at[:, part_of(t, off, w)], RA[n].at[y * 4 + x], "A1", 4 * n + x, dev(t, y, z, c))
            t = wrap(y + k, NY)
            send(b_in.at[:, part_of(t, off, w)], RB[n].at[x * 4 + y], "B1", 4 * n + y, dev(x, t, z, c))

    def two(buf, w, h):
        return buf.at[pl.ds(pl.multiple_of(w * 4 + 2 * h, 2), 2)]

    def f2(n):
        for k in (1, 3, 2):
            t = wrap(x + k, NX)
            recv(RA[n].at[y * 4 + t], "A1", 4 * n + t)
            t = wrap(y + k, NY)
            recv(RB[n].at[x * 4 + t], "B1", 4 * n + t)
        for h in (0, 1):
            for buf, fam, w, to_p, to_m in ((RA[n], "A2", y, yp, ym), (RB[n], "B2", x, xp, xm)):
                a, b = two(buf, w, h), two(buf, w, 1 - h)
                send(a, a, fam, 8 * n + 2 * w + h, to_p)
                send(b, b, fam, 8 * n + 2 * w + 1 - h, to_m)

    views = (("A2", y, NY, yp, ym), ("B2", x, NX, xp, xm))

    def fw(n):
        for (fam, w, size, to_p, to_m), buf in zip(views, (RA[n], RB[n])):
            for h, t, to in ((0, wrap(w - 1, size), to_p), (1, wrap(w + 1, size), to_m)):
                a = two(buf, t, h)
                recv(a, fam, 8 * n + 2 * t + h)
                send(a, a, fam, 8 * n + 2 * t + h, to)

    def norm(n, ta, tb):
        off, w = STEPS[n]
        cs = slice(off, off + w)

        def body(i, _):
            v = (RA[n][ta * 4 + i].astype(F32) - FIN[0:1, cs]) * FIN[1:2, cs]
            TA[rows(slot(i, ta)), cs] = v.astype(BF16)
            v = (RB[n][tb * 4 + i].astype(F32) - FIN[2:3, cs]) * FIN[3:4, cs]
            TB[rows(slot(tb, i)), cs] = v.astype(BF16)
            return 0

        lax.fori_loop(0, 4, body, 0)
        at = pl.ds(pl.multiple_of(ta * 4 * R, 4 * R), 4 * R)
        TT[cs, at] = TA[at, cs].T

    def rest(n):
        norm(n, y, x)
        for (fam, w, size, _, _), buf in zip(views, (RA[n], RB[n])):
            for h, t in ((1, wrap(w - 1, size)), (0, wrap(w + 1, size))):
                recv(two(buf, t, h), fam, 8 * n + 2 * t + h)
        norm(n, wrap(y - 1, NY), wrap(x - 1, NX))
        norm(n, wrap(y + 1, NY), wrap(x + 1, NX))
        for (fam, w, size, _, _), buf in zip(views, (RA[n], RB[n])):
            t = wrap(w + 2, size)
            for h in (0, 1):
                recv(two(buf, t, h), fam, 8 * n + 2 * t + h)
        norm(n, wrap(y + 2, NY), wrap(x + 2, NX))

    def merge(parts, n):
        mean = parts[0][0]
        for m, _ in parts[1:]:
            mean = mean + m
        mean = mean * (1.0 / len(parts))
        total = None
        for m, q in parts:
            d = m - mean
            t = q + n * (d * d)
            total = t if total is None else total + t
        return mean, total

    def st1():
        for k in (2, 1, 3):
            t = wrap(x + k, NX)
            send(S0A.at[t], S1A.at[x], "S1A", x, dev(t, y, z, c))
            t = wrap(y + k, NY)
            send(S0B.at[t], S1B.at[y], "S1B", y, dev(x, t, z, c))
        S1A[x] = S0A[x]
        S1B[y] = S0B[y]

    def st2():
        for k in (1, 3, 2):
            recv(S1A.at[wrap(x + k, NX)], "S1A", wrap(x + k, NX))
            recv(S1B.at[wrap(y + k, NY)], "S1B", wrap(y + k, NY))
        for src, dst, w in ((S1A, S2A, y), (S1B, S2B, x)):
            mean, m2 = merge([(src[k, 0:1, :], src[k, 1:2, :]) for k in range(4)], float(R))
            dst[w, 0:1, :] = mean
            dst[w, 1:2, :] = m2
        for k in (2, 1, 3):
            send(S2A.at[y], S2A.at[y], "S2A", y, dev(x, wrap(y + k, NY), z, c))
            send(S2B.at[x], S2B.at[x], "S2B", x, dev(wrap(x + k, NX), y, z, c))

    def st3():
        for k in (1, 3, 2):
            recv(S2A.at[wrap(y + k, NY)], "S2A", wrap(y + k, NY))
            recv(S2B.at[wrap(x + k, NX)], "S2B", wrap(x + k, NX))
        for v, src in ((0, S2A), (1, S2B)):
            mean, m2 = merge([(src[k, 0:1, :], src[k, 1:2, :]) for k in range(4)], 4.0 * R)
            SC[c, 2 * v:2 * v + 1, :] = mean
            SC[c, 2 * v + 1:2 * v + 2, :] = m2
        send(SC.at[c], SC.at[c], "SC", 0, sib)

    def st4():
        recv(SC.at[o], "SC", 0)
        for v in (0, 1):
            mean, m2 = merge([(SC[k, 2 * v:2 * v + 1, :], SC[k, 2 * v + 1:2 * v + 2, :]) for k in range(2)], 16.0 * R)
            S3[z, 2 * v:2 * v + 1, :] = mean
            S3[z, 2 * v + 1:2 * v + 2, :] = m2
        for k in (4, 3, 5, 2, 6, 1, 7):
            send(S3.at[z], S3.at[z], "S3", z, dev(x, y, wrap(z + k, NZ), c))

    def st5():
        for k in (1, 7, 2, 6, 3, 5, 4):
            recv(S3.at[wrap(z + k, NZ)], "S3", wrap(z + k, NZ))
        for v in (0, 1):
            mean, m2 = merge([(S3[k, 2 * v:2 * v + 1, :], S3[k, 2 * v + 1:2 * v + 2, :]) for k in range(8)], 32.0 * R)
            FIN[2 * v:2 * v + 1, :] = mean
            FIN[2 * v + 1:2 * v + 2, :] = lax.rsqrt(m2 * (1.0 / N) + EPS)

    def comp(n):
        p0, p1 = SETS[n]
        for i, ni, j, nj in RECTS[n]:
            t = jnp.dot(TT[i * E:(i + ni) * E, :], TB[:, j * E:(j + nj) * E], preferred_element_type=F32)
            for a in range(ni):
                for b in range(nj):
                    C2[POS[i + a, j + b]] = t[a * E:(a + 1) * E, b * E:(b + 1) * E].reshape(2, NZ, T, E)
        send(C2.at[p0:p1, o], CR.at[p0:p1], "CX", n, sib)

    zz = lax.broadcasted_iota(jnp.int32, (T, E), 1) - lax.broadcasted_iota(jnp.int32, (T, E), 0)

    def add(n):
        p0, p1 = SETS[n]
        recv(CR.at[p0:p1], "CX", n)

        def body(p, _):
            CO[p] = C2[p, c] + CR[p]
            return 0

        lax.fori_loop(p0, p1, body, 0)
        for p in range(p0, p1):
            i, j = BLOCKS[p]
            if i == j:
                for q in range(NZ):
                    DS[i, q] = jnp.sum(jnp.where(zz == c * 128 + q * T, CO[p, q], 0.0), axis=0, keepdims=True)

    zp2, zm2 = dev(x, y, wrap(z + 2, NZ), c), dev(x, y, wrap(z - 2, NZ), c)
    q4 = (z + 4) % NZ

    def diagonals(n):
        on = sorted(i for i, j in BLOCKS[SETS[n][0]:SETS[n][1]] if i == j)
        return slice(on[0], on[-1] + 1) if on else None

    def rs1(n):
        p0, p1 = SETS[n]
        sl = slice(p0, p1)
        v = CO[sl, q4].astype(BF16)
        ZHP[sl] = v[:, :, :128]
        ZHM[sl] = v[:, :, 128:]
        send(ZHP.at[sl], YHP.at[sl], "ZHP", n, zp2)
        send(ZHM.at[sl], YHM.at[sl], "ZHM", n, zm2)
        for k in (1, 0):
            d = 1 + 2 * k
            Z1P[k, sl] = CO[sl, wrap(z + d, NZ)].astype(BF16)
            send(Z1P.at[k, sl], Y1P.at[k, sl], "Z1P", 2 * n + k, zp)
            Z1M[k, sl] = CO[sl, wrap(z - d, NZ)].astype(BF16)
            send(Z1M.at[k, sl], Y1M.at[k, sl], "Z1M", 2 * n + k, zm)
        ds = diagonals(n)
        if ds is not None:
            for k in range(1, NZ):
                q = wrap(z + k, NZ)
                send(DS.at[ds, q], DV.at[ds, z], "DV", ds.start * NZ + z, dev(x, y, q, c))
            for i in range(ds.start, ds.stop):
                DV[i, z] = DS[i, z]

    def rs2(n):
        sl = slice(*SETS[n])
        recv(YHP.at[sl], "ZHP", n)
        recv(Y1P.at[1, sl], "Z1P", 2 * n + 1)
        v = CO[sl, wrap(z + 2, NZ)] + Y1P[1, sl].astype(F32)
        h = YHP[sl].astype(F32)
        Z2P[sl] = jnp.concatenate([v[:, :, :128] + h, v[:, :, 128:]], axis=2).astype(BF16)
        send(Z2P.at[sl], Y2P.at[sl], "Z2P", n, zp2)
        recv(YHM.at[sl], "ZHM", n)
        recv(Y1M.at[1, sl], "Z1M", 2 * n + 1)
        v = CO[sl, wrap(z - 2, NZ)] + Y1M[1, sl].astype(F32)
        h = YHM[sl].astype(F32)
        Z2M[sl] = jnp.concatenate([v[:, :, :128], v[:, :, 128:] + h], axis=2).astype(BF16)
        send(Z2M.at[sl], Y2M.at[sl], "Z2M", n, zm2)

    def fin(n):
        p0, p1 = SETS[n]
        sl = slice(p0, p1)
        recv(Y1P.at[0, sl], "Z1P", 2 * n)
        recv(Y1M.at[0, sl], "Z1M", 2 * n)
        recv(Y2P.at[sl], "Z2P", n)
        recv(Y2M.at[sl], "Z2M", n)
        ds = diagonals(n)
        if ds is not None:
            for k in range(1, NZ):
                q = wrap(z + k, NZ)
                recv(DV.at[ds, q], "DV", ds.start * NZ + q)
        for p in range(p0, p1):
            i, j = BLOCKS[p]
            cc = CO[p, z] + ((Y1P[0, p].astype(F32) + Y1M[0, p].astype(F32)) + (Y2P[p].astype(F32) + Y2M[p].astype(F32)))
            if i == j:
                dv = DV[i, z]
                for k in range(1, NZ):
                    q = wrap(z + k, NZ)
                    dv = dv + DV[i, q]
                on = jnp.logical_and(zz == c * 128 + z * T, x == y)
                cc = jnp.where(on, dv, cc) * (1.0 / N)
                g = jnp.where(on, -2.0 * (1.0 - cc), (2.0 * OFF_WEIGHT) * cc).astype(BF16)
            else:
                cc = cc * (1.0 / N)
                g = ((2.0 * OFF_WEIGHT) * cc).astype(BF16)
            GS[p, c, z] = g
            prod = g.astype(F32) * cc
            ACC[0, i] = ACC[0, i] + prod
            ACC[1, j] = ACC[1, j] + prod
        src = GS.at[sl, c, z]
        ways_ = ((1, zp2), (3, zm2), (0, zp), (2, zm)) if n in SHORT else ((0, zp), (2, zm))
        for k, to in ways_:
            send(src, src, "GF", 8 * n + k, to)

    def ag1(n):
        sl = slice(*SETS[n])
        for k, q, to in ((0, wrap(z - 1, NZ), zp), (2, wrap(z + 1, NZ), zm)):
            src = GS.at[sl, c, q]
            recv(src, "GF", 8 * n + k)
            send(src, src, "GF", 8 * n + k + 1, to)

    lanes_p, lanes_m = slice(0, 128), slice(128, 256)

    def ag2(n):
        sl = slice(*SETS[n])
        for k, q, to, to2, lanes in ((1, wrap(z - 2, NZ), zp, zp2, lanes_p), (3, wrap(z + 2, NZ), zm, zm2, lanes_m)):
            src = GS.at[sl, c, q]
            recv(src, "GF", 8 * n + k)
            half = GS.at[sl, c, q, :, lanes]
            send(half, half, "GH", 2 * n + k // 2, to2)
            send(src, src, "GF", 8 * n + 4 + k, to)

    def gx(n):
        sl = slice(*SETS[n])
        near = ((0, wrap(z - 1, NZ)), (2, wrap(z + 1, NZ))) if n in SHORT else ()
        for k, q in near + ((5, wrap(z - 3, NZ)), (7, wrap(z + 3, NZ))):
            recv(GS.at[sl, c, q], "GF", 8 * n + k)
        recv(GS.at[sl, c, q4, :, lanes_p], "GH", 2 * n)
        recv(GS.at[sl, c, q4, :, lanes_m], "GH", 2 * n + 1)
        send(GS.at[sl, c], GS.at[sl, c], "GX", n, sib)

    def gx_wait(n):
        sl = slice(*SETS[n])
        recv(GS.at[sl, o], "GX", n)

    def mom1():
        for i in range(4):
            r = jnp.sum(ACC[0, i], axis=1, keepdims=True)
            MS[c, 0:1, i * E:(i + 1) * E] = jnp.sum(jnp.where(zz == c * 128 + z * T, r, 0.0), axis=0, keepdims=True)
            MS[c, 1:2, i * E:(i + 1) * E] = jnp.sum(ACC[1, i], axis=0, keepdims=True)
        send(MS.at[c], MS.at[c], "MS", 0, sib)

    def mom1b():
        recv(MS.at[o], "MS", 0)
        MO[z] = MS[0] + MS[1]
        for k in (4, 3, 5, 2, 6, 1, 7):
            send(MO.at[z], MO.at[z], "MO", z, dev(x, y, wrap(z + k, NZ), c))

    def mom2():
        for k in (1, 7, 2, 6, 3, 5, 4):
            recv(MO.at[wrap(z + k, NZ)], "MO", wrap(z + k, NZ))
        for r, dst in ((0, MA.at[y]), (1, MB.at[x])):
            t = MO[0, r:r + 1, :]
            for k in range(1, NZ):
                t = t + MO[k, r:r + 1, :]
            dst[...] = t
        for k in (2, 1, 3):
            send(MA.at[y], MA.at[y], "MA", y, dev(x, wrap(y + k, NY), z, c))
            send(MB.at[x], MB.at[x], "MB", x, dev(wrap(x + k, NX), y, z, c))

    def mom3():
        for k in (1, 3, 2):
            recv(MA.at[wrap(y + k, NY)], "MA", wrap(y + k, NY))
            recv(MB.at[wrap(x + k, NX)], "MB", wrap(x + k, NX))
        FIN[4:5, :] = ((MA[0] + MA[1]) + (MA[2] + MA[3])) * SCALE
        FIN[5:6, :] = ((MB[0] + MB[1]) + (MB[2] + MB[3])) * SCALE

    def part(v, u, first, w):
        h = slice(0, 2) if first else slice(2, 4)
        return PB.at[v, u, w, h] if v == 0 else PB.at[v, u, h, w]

    def ways(v):
        return (y, NY, yp, ym) if v == 0 else (x, NX, xp, xm)

    def bw1(v, u):
        t = None
        for k in range(4):
            if v == 0:
                g = GS[POS[u, k]].reshape(E, E)
                d = lax.dot_general(TB[:, k * E:(k + 1) * E], g, (((1,), (1,)), ((), ())), preferred_element_type=F32)
            else:
                g = GS[POS[k, u]].reshape(E, E)
                d = jnp.dot(TA[:, k * E:(k + 1) * E], g, preferred_element_type=F32)
            t = d if t is None else t + d
        PB[v, u] = (SCALE * t).astype(BF16).reshape(4, 4, R, E)
        pos, n, to_p, to_m = ways(v)
        i = 8 * v + 2 * u
        send(part(v, u, True, wrap(pos + 2, n)), BH.at[v, u, 0], "BH", i, to_p)
        send(part(v, u, False, wrap(pos + 2, n)), BH.at[v, u, 1], "BH", i + 1, to_m)
        send(part(v, u, False, wrap(pos + 1, n)), BF.at[v, u, 0, 2:4], "BF", 2 * i + 1, to_p)
        send(part(v, u, True, wrap(pos - 1, n)), BF.at[v, u, 1, 0:2], "BF", 2 * i + 2, to_m)

    def bw2(v, u):
        pos, n, to_p, to_m = ways(v)
        i = 8 * v + 2 * u
        recv(BH.at[v, u, 0], "BH", i)
        src = part(v, u, True, wrap(pos + 1, n))
        src[...] = (src[...].astype(F32) + BH[v, u, 0].astype(F32)).astype(BF16)
        send(src, BF.at[v, u, 0, 0:2], "BF", 2 * i, to_p)
        recv(BH.at[v, u, 1], "BH", i + 1)
        src = part(v, u, False, wrap(pos - 1, n))
        src[...] = (src[...].astype(F32) + BH[v, u, 1].astype(F32)).astype(BF16)
        send(src, BF.at[v, u, 1, 2:4], "BF", 2 * i + 3, to_m)

    def out(v, u):
        i = 2 * (8 * v + 2 * u)
        for k in range(4):
            recv(BF.at[v, u, k // 2, (k % 2) * 2:(k % 2) * 2 + 2], "BF", i + k)
        w = slice(u * E, (u + 1) * E)
        for r in (2, 1, 3, 0):
            if v == 0:
                t = wrap(x + r, NX)
                mine_ = PB[0, u, y, t]
                norm = TA[rows(slot(t, y)), w]
                m, rs = FIN[4:5, w], FIN[1:2, w]
                dst = ga.at[:, pl.ds(pl.multiple_of(x * W + u * E, E), E)]
                fam, at, to = "OA", 4 * u + x, dev(t, y, z, c)
            else:
                t = wrap(y + r, NY)
                mine_ = PB[1, u, t, x]
                norm = TB[rows(slot(x, t)), w]
                m, rs = FIN[5:6, w], FIN[3:4, w]
                dst = gb.at[:, pl.ds(pl.multiple_of(y * W + u * E, E), E)]
                fam, at, to = "OB", 4 * u + y, dev(x, t, z, c)
            back = mine_.astype(F32) + (BF[v, u, 0, t].astype(F32) + BF[v, u, 1, t].astype(F32))
            grad = (rs * (back - norm.astype(F32) * m)).astype(BF16)
            if r:
                buf = SA if v == 0 else SB
                buf[u, r] = grad
                send(buf.at[u, r], dst, fam, at, to)
            else:
                dst[...] = grad

    ACC[...] = jnp.zeros_like(ACC)
    st1()
    f1(0)
    f1(1)
    f1(2)
    st2()
    f2(0)
    st3()
    st4()
    fw(0)
    f2(1)
    f2(2)
    st5()
    rest(0)
    comp(0)
    fw(1)
    add(0)
    rs1(0)
    fw(2)
    rest(1)
    comp(1)
    rs2(0)
    rest(2)
    comp(2)
    add(1)
    rs1(1)
    comp(3)
    comp(4)
    add(2)
    rs1(2)
    comp(5)
    add(3)
    rs1(3)
    add(4)
    rs1(4)
    rs2(1)
    add(5)
    comp(6)
    rs1(5)
    rs2(2)
    fin(0)
    add(6)
    rs1(6)
    rs2(4)
    rs2(3)
    fin(1)
    ag1(0)
    fin(2)
    rs2(6)
    rs2(5)
    ag1(1)
    fin(4)
    ag2(0)
    fin(3)
    ag2(1)
    ag2(2)
    ag1(4)
    fin(5)
    gx(0)
    fin(6)
    ag2(3)
    gx(1)
    gx_wait(0)
    gx(2)
    ag2(4)
    mom1()
    gx_wait(1)
    gx_wait(2)
    bw1(1, 0)
    ag2(6)
    bw1(0, 0)
    ag2(5)
    gx(3)
    gx(4)
    gx_wait(3)
    mom1b()
    gx_wait(4)
    bw1(0, 1)
    bw2(1, 0)
    gx(6)
    bw1(1, 1)
    gx(5)
    gx_wait(6)
    bw1(0, 3)
    bw1(1, 3)
    gx_wait(5)
    bw1(0, 2)
    bw1(1, 2)
    bw2(0, 0)
    mom2()
    bw2(0, 3)
    bw2(0, 2)
    bw2(0, 1)
    bw2(1, 1)
    bw2(1, 3)
    bw2(1, 2)
    mom3()
    out(1, 0)
    out(0, 0)
    out(0, 3)
    out(1, 3)
    out(0, 2)
    out(1, 1)
    out(1, 2)
    out(0, 1)
    for u in range(4):
        for k in (1, 3, 2):
            t = wrap(x + k, NX)
            recv(ga.at[:, pl.ds(pl.multiple_of(t * W + u * E, E), E)], "OA", 4 * u + t)
            t = wrap(y + k, NY)
            recv(gb.at[:, pl.ds(pl.multiple_of(t * W + u * E, E), E)], "OB", 4 * u + t)
    for cp in sent:
        cp.wait_send()


def local(view_a, view_b):
    V = pltpu.VMEM
    scratch = [
        V((R, D), BF16), V((R, D), BF16),
        *[V((16, R, w), BF16) for _ in range(2) for _, w in STEPS],
        V((16 * R, W), BF16), V((16 * R, W), BF16),
        V((4, 2, W), F32), V((4, 2, W), F32),
        V((4, 2, W), F32), V((4, 2, W), F32),
        V((4, 2, W), F32), V((4, 2, W), F32),
        V((2, 4, W), F32), V((8, 4, W), F32), V((6, W), F32),
        V((W, W), BF16),
        V((16, 2, NZ, T, E), F32), V((16, NZ, T, E), F32), V((16, NZ, T, E), F32),
        V((2, 16, T, E), BF16), V((2, 16, T, E), BF16),
        V((16, T, 128), BF16), V((16, T, 128), BF16),
        V((16, T, E), BF16), V((16, T, E), BF16),
        V((2, 16, T, E), BF16), V((2, 16, T, E), BF16),
        V((16, T, 128), BF16), V((16, T, 128), BF16),
        V((16, T, E), BF16), V((16, T, E), BF16),
        V((4, NZ, 1, E), F32), V((4, NZ, 1, E), F32),
        V((16, 2, NZ, T, E), BF16), V((2, 4, T, E), F32),
        V((2, 2, W), F32), V((8, 2, W), F32), V((4, 1, W), F32), V((4, 1, W), F32),
        V((2, 4, 4, 4, R, E), BF16),
        V((2, 4, 2, 2, R, E), BF16), V((2, 4, 2, 4, R, E), BF16),
        V((4, 4, R, E), BF16), V((4, 4, R, E), BF16),
        pltpu.SemaphoreType.DMA((N_SEND,)),
        pltpu.SemaphoreType.DMA((N_RECV,)),
    ]
    out = pltpu.VMEM((R, D), BF16)
    return tuple(pl.pallas_call(
        kernel,
        out_shape=(out, out),
        in_specs=[pl.BlockSpec(memory_space=pl.ANY)] * 2,
        out_specs=(pl.BlockSpec(memory_space=pltpu.VMEM),) * 2,
        scratch_shapes=scratch,
        compiler_params=pltpu.CompilerParams(
            collective_id=0, has_side_effects=True, vmem_limit_bytes=56 * 1024 * 1024),
    )(view_a, view_b))


def solution(mesh):
    spec = P(("dp", "mp"), None)
    return jax.shard_map(local, mesh=mesh, in_specs=(spec, spec), out_specs=(spec, spec), check_vma=False)
```
